512 devices in a mesh: band: 16 (over y, core), ga: 32 (over z, x).
Axes of the slice: x: 4, y: 8, z: 8, core: 2. Of those that a mesh axis runs over, the one named last changes fastest.
Arguments:
- coef_x: float32 [16, 3072, 256], P('band', 'ga'), may hold values from -26 to 26
- coef_w: float32 [16, 3072, 256], P('band', 'ga'), may hold values from -26 to 26
- coef_p: float32 [16, 3072, 256], P('band', 'ga'), may hold values from -26 to 26
- hcoef_x: float32 [16, 3072, 256], P('band', 'ga'), may hold values from -110 to 110
- hcoef_p: float32 [16, 3072, 256], P('band', 'ga'), may hold values from -110 to 110
- potential: float32 [128, 128, 128], P('ga'), may hold values from -5 to 5
- stick_column: int32 [3072], replicated, may hold values from 0 to 16383, as said below
- sphere_mask: int32 [3072, 128], P('ga'), may hold values from 0 to 1, as said below
Outputs:
- h_wave: float32 [16, 3072, 256], P('band', 'ga')
- reduced: float32 [96, 96], replicated
The draws below stay inside these ranges and needn't reach their ends.
Inputs may be any that keep to these rules, and one draw needn't show every extreme that they name: `stick_column`: distinct grid columns: the 3072 columns of smallest f(y)^2 + f(z)^2, ties on the outermost circle broken at random, in random order. `sphere_mask`: a sphere: ones exactly where f(k)^2 + f(y_s)^2 + f(z_s)^2 is at most the largest f(y_s)^2 + f(z_s)^2 over all sticks.
All inputs are finite; a program needn't handle non-finite values.
Results may differ from the reference program's by a relative error of at most 0.00012.
Values sent between devices are 32-bit elements; how exact they have to be, the bound alone decides.
A program may use at most 128 MiB of HBM per device.

```python
import math
import jax
import jax.numpy as jnp
from jax import lax

NG = 128
BANDS = 16
NSTICKS = 3072


def shared_part(key):
    return jnp.clip(jax.random.normal(key, (NSTICKS, 2 * NG), jnp.float32), -4.0, 4.0)


def vectors(key, tag):
    common = shared_part(key)
    own = jax.random.fold_in(key, tag)
    base = jnp.clip(jax.random.normal(own, (BANDS, NSTICKS, 2 * NG), jnp.float32), -4.0, 4.0)
    weight = jax.random.uniform(jax.random.fold_in(own, 50), (BANDS,), jnp.float32, -0.6, 0.6)
    return base + weight[:, None, None] * common[None]


def images(key, tag):
    start = vectors(key, tag)
    own = jax.random.fold_in(key, tag + 10)
    energy = jnp.exp(jax.random.uniform(own, (BANDS,), jnp.float32, math.log(0.5), math.log(4.0)))
    noise = jnp.clip(jax.random.normal(jax.random.fold_in(own, 1), start.shape, jnp.float32), -4.0, 4.0)
    return energy[:, None, None] * start + 0.3 * noise


def folded_ints():
    k = jnp.arange(NG, dtype=jnp.int32)
    return jnp.where(k < NG // 2, k, k - NG)


def disk_columns(key):
    key = jax.random.fold_in(key, 9)
    fold = folded_ints()
    cols = jnp.arange(NG * NG, dtype=jnp.int32)
    fy = fold[cols // NG]
    fz = fold[cols % NG]
    radial = fy * fy + fz * fz
    breaker = jax.random.permutation(key, NG * NG).astype(jnp.int32)
    score = radial * 65536 + breaker
    chosen = jnp.argsort(score)[:NSTICKS].astype(jnp.int32)
    placing = jax.random.permutation(jax.random.fold_in(key, 1), NSTICKS)
    columns = chosen[placing].astype(jnp.int32)
    return (columns, radial[columns])


def draw_coef_x(key, part):
    return vectors(key, 1)


def draw_coef_w(key, part):
    return vectors(key, 2)


def draw_coef_p(key, part):
    return vectors(key, 3)


def draw_hcoef_x(key, part):
    return images(key, 1)


def draw_hcoef_p(key, part):
    return images(key, 3)


def draw_stick_column(key, part):
    columns, radial = disk_columns(key)
    return columns


def draw_sphere_mask(key, part):
    columns, radial = disk_columns(key)
    fold = folded_ints()
    limit = jnp.max(radial)
    return (fold[None, :] * fold[None, :] + radial[:, None] <= limit).astype(jnp.int32)


def block_levels(stream_key, dims, pieces, low, largest):
    def one(dim, shards_of):
        draws = jax.random.uniform(jax.random.fold_in(jax.random.fold_in(stream_key, 6), dim), (shards_of,), jnp.float32, low / len(pieces), largest / len(pieces))
        return jnp.repeat(jnp.exp(draws), dims[dim] // shards_of).reshape((-1,) + (1,) * (len(dims) - dim - 1))

    level = one(*pieces[0])
    for cut in pieces[1:]:
        level = level * one(*cut)
    return level


def gaussian(own_key, dims, scale, reach, split=(), kind=jnp.bfloat16):
    level = block_levels(own_key, dims, split, -0.22, 0.18) if split else 1.0
    entries = jax.random.normal(own_key, dims, jnp.float32) * scale * level
    return jnp.minimum(jnp.maximum(entries, -reach), reach).astype(kind)


def setup_inputs(seed: int = 0) -> dict:
    splits = jax.random.split(jax.random.key(seed), 9)
    return {
        "coef_x": draw_coef_x(jax.random.fold_in(splits[8], 71), 0),
        "coef_w": draw_coef_w(jax.random.fold_in(splits[8], 71), 0),
        "coef_p": draw_coef_p(jax.random.fold_in(splits[8], 71), 0),
        "hcoef_x": draw_hcoef_x(jax.random.fold_in(splits[8], 71), 0),
        "hcoef_p": draw_hcoef_p(jax.random.fold_in(splits[8], 71), 0),
        "potential": gaussian(splits[5], (NG, NG, NG), 1.0, 5.0, ((0, 32),), jnp.float32),
        "stick_column": draw_stick_column(jax.random.fold_in(splits[8], 71), 0),
        "sphere_mask": draw_sphere_mask(jax.random.fold_in(splits[8], 71), 0),
    }


def folded(count):
    k = jnp.arange(count, dtype=jnp.int32)
    return jnp.where(k < count // 2, k, k - count)

def kinetic_table(columns, count):
    fx = folded(count).astype(jnp.float32)
    fy = folded(count)[columns // count].astype(jnp.float32)
    fz = folded(count)[columns % count].astype(jnp.float32)
    factor = 0.5 * (2.0 * math.pi / count) ** 2
    return factor * (fx[None, :] ** 2 + (fy ** 2 + fz ** 2)[:, None])

def reference(coef_x, coef_w, coef_p, hcoef_x, hcoef_p, potential, stick_column, sphere_mask):
    count = potential.shape[0]
    nst = stick_column.shape[0]
    maskf = sphere_mask.astype(jnp.float32)
    mask_two = jnp.concatenate([maskf, maskf], axis=1)
    kinetic = kinetic_table(stick_column, count)
    kin_two = jnp.concatenate([kinetic, kinetic], axis=1)
    total = float(count) ** 3

    def apply_one(wave):
        wave = wave * mask_two
        comp = wave[:, :count] + 1j * wave[:, count:]
        grid = jnp.zeros((count, count * count), comp.dtype)
        grid = grid.at[:, stick_column].set(comp.T).reshape(count, count, count)
        field = jnp.fft.ifftn(grid) * total
        back = jnp.fft.fftn(potential * field) / total
        sticks = back.reshape(count, count * count)[:, stick_column].T
        joined = jnp.concatenate([jnp.real(sticks), jnp.imag(sticks)], axis=1)
        return mask_two * (kin_two * wave + joined)
    h_wave = lax.map(apply_one, coef_w)
    masked = [v * mask_two[None] for v in (coef_x, coef_w, coef_p, hcoef_x, hcoef_p)]
    span = jnp.concatenate([masked[0], masked[1], masked[2]], axis=0).reshape(3 * coef_w.shape[0], -1)
    image = jnp.concatenate([masked[3], h_wave, masked[4]], axis=0).reshape(3 * coef_w.shape[0], -1)

    def turned(v):
        shaped = v.reshape(v.shape[0], nst, 2, count)
        return jnp.concatenate([shaped[:, :, 1], -shaped[:, :, 0]], axis=2).reshape(v.shape[0], -1)
    hi = lax.Precision.HIGHEST
    re_h = jnp.dot(span, image.T, precision=hi)
    im_h = jnp.dot(span, turned(image).T, precision=hi)
    re_s = jnp.dot(span, span.T, precision=hi)
    im_s = jnp.dot(span, turned(span).T, precision=hi)
    big_h = jnp.block([[re_h, -im_h], [im_h, re_h]])
    big_s = jnp.block([[re_s, -im_s], [im_s, re_s]])
    lower = jnp.linalg.cholesky(big_s)
    first = jax.scipy.linalg.solve_triangular(lower, big_h, lower=True)
    reduced = jax.scipy.linalg.solve_triangular(lower, first.T, lower=True).T
    return (h_wave, reduced)
```

```python
import functools
import math

import jax
import jax.numpy as jnp
import numpy as np
from jax import lax
from jax.experimental import pallas as pl
from jax.experimental.pallas import tpu as pltpu
from jax.sharding import PartitionSpec as P

F32 = jnp.float32
BF16 = jnp.bfloat16
HI = lax.Precision.HIGHEST
ROWS = 8
LANES = 128
NT = (((1,), (1,)), ((), ()))
NN = (((1,), (0,)), ((), ()))
GA_OUT, GA_BACK, SPREAD, TILES, TILE_SUM, TILE_ALL, LATE, LATE_GA, LATE_BAND = range(9)


def dot(a, b, dims=NN, precision=HI):
    return lax.dot_general(a, b, dims, precision=precision, preferred_element_type=F32)


def tables(n, planes):
    half, quarter = n // 2, n // 4
    lane = np.arange(n)
    is_real = (lane < quarter) | (lane >= n - quarter)
    k_of = np.where(is_real, lane, (lane - half) % n)
    fold_k = np.where(k_of < half, k_of, k_of - n)
    groups = n // planes
    x = (np.arange(groups)[:, None, None] * planes + np.arange(planes)[None, None, :]) + np.zeros((1, 2, 1), int)
    part = np.arange(2)[None, :, None] + np.zeros((groups, 1, planes), int)
    x, part = x.reshape(-1), part.reshape(-1)

    def angle(a, b):
        return 2.0 * math.pi * ((a[:, None] * b[None, :]) % n) / n

    th = angle(x, fold_k)
    c, s = np.cos(th), np.sin(th)
    pr = part[:, None] == 0
    ir = is_real[None, :]
    forward = np.where(pr, np.where(ir, c, -s), np.where(ir, s, c))
    inverse = np.where(pr, np.where(ir, c, -s), np.where(ir, s, c)) / float(n) ** 3
    small = np.arange(half)
    small = np.where(small < quarter, small, small - half)
    full = np.arange(n)
    th = angle(small, full)
    c, s = np.cos(th), np.sin(th)
    z_plus = np.concatenate([c, s], axis=1)
    y_plus = np.block([[c.T, -s.T], [s.T, c.T]])
    y_minus = np.block([[c, s], [-s, c]])
    z_real = np.concatenate([c.T, s.T], axis=0)
    z_imag = np.concatenate([-s.T, c.T], axis=0)
    z_minus = np.concatenate([z_real, z_real, z_imag, z_imag], axis=1)
    fx2 = (fold_k.astype(np.float64) ** 2)[None, :]
    return [np.asarray(t, np.float32) for t in (forward, inverse, z_plus, y_plus, y_minus, z_minus, fx2)]


def kernel(n, nb, ng, sd, planes,
           coef_w_in, mask_in, forward_in, hcoef_x_in, hcoef_p_in, coef_x_in, coef_p_in, cols_in, fx2_in,
           z_plus_in, y_plus_in, pot_in, y_minus_in, z_minus_in, inverse_in,
           h_out, red_out,
           coef_w, mask, forward, hcoef_x, hcoef_p, coef_x, coef_p, cols, fx2,
           z_plus, y_plus, pot, y_minus, z_minus, inverse,
           src, ga_src, ga_in, hot, back_src, back_in, spread, own, ss2, early, tiles, tile_sum, tile_in,
           tile_all, hw, late, late_part, late_in, late_sum, late_all, big_a, big_b, kin_ref, gauge, q_cols, send, recv, load):
    half, quarter = n // 2, n // 4
    rb = 2 * planes
    sp = hot.shape[2]
    cells = rb * half
    nslice = sd // ROWS
    width = 3 * nb
    ntile = 5 * nb // ROWS
    b = lax.axis_index("band")
    g = lax.axis_index("ga")
    lane = lax.broadcasted_iota(jnp.int32, (1, n), 1)
    real_lane = (lane < quarter) | (lane >= n - quarter)
    sign = jnp.where(real_lane, -1.0, 1.0).astype(F32)

    def swap(v):
        return pltpu.roll(v, half, 1)

    def pack(ref):
        v = ref[0]
        return jnp.where(real_lane, v[:, :n], swap(v[:, n:]))

    def rows(i, count=ROWS):
        return pl.ds(pl.multiple_of(i * count, count), count)

    def each(count, me, body):
        def step(d, carry):
            body(lax.rem(me + d, count))
            return carry
        lax.fori_loop(1, count, step, 0)

    def push(src_ref, dst_ref, phase, where):
        pltpu.make_async_remote_copy(
            src_ref=src_ref, dst_ref=dst_ref, send_sem=send.at[phase], recv_sem=recv.at[phase],
            device_id=where, device_id_type=pl.DeviceIdType.MESH).start()

    def wait_rows(ref, count, sem):
        piece = ref.at[pl.ds(0, count)]
        pltpu.make_async_copy(piece, piece, sem).wait()

    def wait_from(ref, sources, size, sem):
        if sources >= nb:
            wait_rows(ref, (nb - 1) * size, sem)
        else:
            @pl.when(b < sources)
            def _():
                wait_rows(ref, (sources - 1) * size, sem)

            @pl.when(b >= sources)
            def _():
                wait_rows(ref, sources * size, sem)

    held = [coef_w, mask, forward, hcoef_x, hcoef_p, coef_x, coef_p, cols, fx2,
            z_plus, y_plus, pot, y_minus, z_minus, inverse]
    given = [coef_w_in, mask_in, forward_in, hcoef_x_in, hcoef_p_in, coef_x_in, coef_p_in, cols_in, fx2_in,
             z_plus_in, y_plus_in, pot_in, y_minus_in, z_minus_in, inverse_in]
    loads = [pltpu.make_async_copy(a, v, load.at[i]) for i, (a, v) in enumerate(zip(given, held))]
    for copy in loads:
        copy.start()

    barrier = pltpu.get_barrier_semaphore()

    def greet_ga(p):
        pl.semaphore_signal(barrier, inc=1, device_id=(b, p), device_id_type=pl.DeviceIdType.MESH)

    def greet_band(p):
        pl.semaphore_signal(barrier, inc=1, device_id=(p, g), device_id_type=pl.DeviceIdType.MESH)

    each(ng, g, greet_ga)
    each(nb, b, greet_band)

    for copy in loads[:3]:
        copy.wait()
    m = mask[...].astype(F32)
    pm = jnp.where(real_lane, m, swap(m))
    w = pack(coef_w) * pm
    src[3] = w
    wide = jnp.concatenate([w, jnp.zeros((sp - sd, n), F32)], axis=0) if sp > sd else w
    ga_src[...] = dot(forward[...], wide, NT)
    for copy in loads[3:7]:
        copy.wait()
    src[0] = pack(hcoef_x) * pm
    src[1] = pack(hcoef_p) * pm
    src[2] = pack(coef_x) * pm
    src[4] = pack(coef_p) * pm

    pl.semaphore_wait(barrier, ng + nb - 2)

    def send_ga(p):
        push(ga_src.at[rows(p, rb)], ga_in.at[rows(g, rb)], GA_OUT, (b, p))

    each(ng, g, send_ga)
    ga_in[rows(g, rb), :] = ga_src[rows(g, rb), :]

    def send_spread(p):
        @pl.when(p < nslice)
        def _():
            push(src.at[:, rows(p), :], spread.at[:, rows(b), :], SPREAD, (p, g))

    each(nb, b, send_spread)

    @pl.when(b < nslice)
    def _():
        spread[:, rows(b), :] = src[:, rows(b), :]

    for copy in loads[7:9]:
        copy.wait()

    fourth = n // 4
    strided = [cols[pl.ds(t, ng // 4, stride=3), :] for t in range(3)]
    lane32 = lax.broadcasted_iota(jnp.int32, (1, n), 1)
    q_cols[0] = strided[0]
    q_cols[1] = jnp.where(lane32 < fourth, pltpu.roll(strided[0], fourth, 1), pltpu.roll(strided[1], fourth, 1))
    q_cols[2] = jnp.where(lane32 < half, pltpu.roll(strided[1], half, 1), pltpu.roll(strided[2], half, 1))
    q_cols[3] = pltpu.roll(strided[2], 3 * fourth, 1)

    def cols_of(q):
        return q_cols[lax.rem(q, 4), pl.ds(q // 4, 1), :]

    def make_hot(q, carry):
        zc = cols_of(q) & (half - 1)
        one = jnp.where(lax.broadcasted_iota(jnp.int32, (half, sp), 0) == zc, 1.0, 0.0).astype(BF16)
        hot[q] = jnp.concatenate([one, one], axis=0)
        return carry

    lax.fori_loop(0, ng, make_hot, 0)

    def folded(v):
        return jnp.where(v < half, v, v - n)

    mine = cols_of(g)
    fy, fz = folded(mine // n), folded(mine & (n - 1))
    radial = jnp.broadcast_to((fy * fy + fz * fz).astype(F32), (n, sp)).T[:sd]
    kin_ref[...] = 0.5 * (2.0 * math.pi / n) ** 2 * (fx2[...] + radial)

    wait_rows(ga_in, (ng - 1) * rb, recv.at[GA_OUT])

    def y_hot(q):
        yc = (cols_of(q) // n) & (half - 1)
        return lax.broadcasted_iota(jnp.int32, (half, sp), 0) == yc

    group = 4 if ng % 4 == 0 else 2

    def scatter(i, acc):
        left, right = [], []
        for t in range(group):
            q = i * group + t
            v = ga_in[rows(q, rb), :]
            high = v.astype(BF16).astype(F32)
            low = v - high
            here = y_hot(q)[None]
            one = hot[q][:half]
            for piece in (high, low):
                spreadout = jnp.where(here, piece[:, None, :], 0.0).reshape(cells, sp)
                left.append(spreadout.astype(BF16))
                right.append(one)
        return acc + dot(jnp.concatenate(left, axis=1), jnp.concatenate(right, axis=1), NT, None)

    grid = lax.fori_loop(0, ng // group, scatter, jnp.zeros((cells, half), F32))

    for copy in loads[9:]:
        copy.wait()
    mid = planes * half
    turned = dot(grid, z_plus[...])
    f_re = turned[:mid, :n] - turned[mid:, n:]
    f_im = turned[:mid, n:] + turned[mid:, :n]
    stacked = jnp.concatenate(
        [jnp.concatenate([f_re[j * half:(j + 1) * half], f_im[j * half:(j + 1) * half]], axis=0)
         for j in range(planes)], axis=1)
    field = dot(y_plus[...], stacked)
    potential = jnp.concatenate([pot[j] for j in range(planes)], axis=1)
    product = jnp.concatenate([field[:n] * potential, field[n:] * potential], axis=0)
    product = dot(y_minus[...], product)
    product = jnp.concatenate(
        [jnp.concatenate([product[:half, j * n:(j + 1) * n], product[half:, j * n:(j + 1) * n]], axis=1)
         for j in range(planes)], axis=0)
    product = dot(product, z_minus[...])
    product = jnp.concatenate([product[:, :n], product[:, n:]], axis=0)
    high = product.astype(BF16).astype(F32)
    low = product - high
    both = jnp.where(lax.broadcasted_iota(jnp.int32, (1, n), 1) < half, high, low).astype(BF16)

    def gather(i, carry):
        pair = jnp.concatenate([hot[2 * i], hot[2 * i + 1]], axis=1)
        found = dot(both, pair, NN, None)
        for t in range(2):
            q = 2 * i + t
            here = y_hot(q)[None]
            part = found[:, t * sp:(t + 1) * sp].reshape(rb, half, sp)
            back_src[rows(q, rb), :] = jnp.sum(jnp.where(here, part, 0.0), axis=1)

            @pl.when(q != g)
            def _():
                push(back_src.at[rows(q, rb)], back_in.at[rows(g, rb)], GA_BACK, (b, q))
        return carry

    lax.fori_loop(0, ng // 2, gather, 0)
    back_in[rows(g, rb), :] = back_src[rows(g, rb), :]

    @pl.when(b < nslice)
    def _():
        piece = spread.at[0:5, pl.ds(0, (nb - 1) * ROWS)]
        pltpu.make_async_copy(piece, piece, recv.at[SPREAD]).wait()
        left, right = [], []
        for r in range(ROWS):
            vec = [spread[a, pl.ds(r, nb, stride=ROWS), :] for a in range(5)]
            s = jnp.concatenate(vec[2:], axis=0)
            left.append(jnp.concatenate(vec, axis=0))
            right.append(jnp.concatenate([s, swap(s) * sign], axis=0))
        right = jnp.concatenate(right, axis=1)
        ss2[...] = right
        early[:, :2 * width] = dot(jnp.concatenate(left, axis=1), right, NT)

        def send_tile(p):
            @pl.when(p < ntile)
            def _():
                push(early.at[rows(p)], tiles.at[rows(b)], TILES, (p, g))

        each(nb, b, send_tile)

        @pl.when(b < ntile)
        def _():
            tiles[rows(b), :] = early[rows(b), :]

    wait_rows(back_in, (ng - 1) * rb, recv.at[GA_BACK])
    local = dot(back_in[...].T, inverse[...])[:sd]
    h = pm * (kin_ref[...] * w + local)
    hw[...] = h

    def send_late(p):
        @pl.when(p < nslice)
        def _():
            push(hw.at[rows(p)], late.at[rows(b)], LATE, (p, g))

    each(nb, b, send_late)

    @pl.when(b < nslice)
    def _():
        late[rows(b), :] = hw[rows(b), :]

    h_out[0, :, :n] = jnp.where(real_lane, h, 0.0)
    h_out[0, :, n:] = jnp.where(real_lane, swap(h), 0.0)

    @pl.when(b < ntile)
    def _():
        wait_from(tiles, nslice, ROWS, recv.at[TILES])
        tile_sum[...] = jnp.sum(tiles[:nslice * ROWS, :].reshape(nslice, ROWS, LANES), axis=0)

        def send_sum(p):
            push(tile_sum, tile_in.at[rows(g)], TILE_SUM, (b, p))

        each(ng, g, send_sum)
        tile_in[rows(g), :] = tile_sum[...]

    @pl.when(b < nslice)
    def _():
        wait_rows(late, (nb - 1) * ROWS, recv.at[LATE])
        left = jnp.concatenate([late[pl.ds(r, nb, stride=ROWS), :] for r in range(ROWS)], axis=1)
        late_part[:, :2 * width] = dot(left, ss2[...], NT)

        def send_part(p):
            push(late_part, late_in.at[rows(g, nb)], LATE_GA, (b, p))

        each(ng, g, send_part)
        late_in[rows(g, nb), :] = late_part[...]

    @pl.when(b < ntile)
    def _():
        wait_rows(tile_in, (ng - 1) * ROWS, recv.at[TILE_SUM])
        tile_all[rows(b), :] = jnp.sum(tile_in[...].reshape(ng, ROWS, LANES), axis=0)

        def send_all(p):
            push(tile_all.at[rows(b)], tile_all.at[rows(b)], TILE_ALL, (p, g))

        each(nb, b, send_all)

    @pl.when(b < nslice)
    def _():
        wait_rows(late_in, (ng - 1) * nb, recv.at[LATE_GA])
        late_all[rows(b, nb), :] = jnp.sum(late_in[:ng * nb, :].reshape(ng, nb, LANES), axis=0)

        def send_whole(p):
            push(late_all.at[rows(b, nb)], late_all.at[rows(b, nb)], LATE_BAND, (p, g))

        each(nb, b, send_whole)

    wait_from(tile_all, ntile, ROWS, recv.at[TILE_ALL])

    def full(top):
        return jnp.concatenate(
            [top, jnp.concatenate([-top[:, width:2 * width], top[:, :width]], axis=1)], axis=0)

    size = 2 * width
    big_a[...] = full(tile_all[2 * nb:, :size])
    here = lax.broadcasted_iota(jnp.int32, (size, size), 0)
    there = lax.broadcasted_iota(jnp.int32, (size, size), 1)
    big_b[...] = jnp.where(here == there, 1.0, 0.0).astype(F32)
    row_id = lax.broadcasted_iota(jnp.int32, (size, 1), 0)
    col_id = lax.broadcasted_iota(jnp.int32, (1, size), 1)

    def eliminate(j, carry):
        a, inv = big_a[...], big_b[...]
        row, inv_row = big_a[pl.ds(j, 1), :], big_b[pl.ds(j, 1), :]
        pivot = jnp.sum(jnp.where(col_id == j, row, 0.0), axis=1, keepdims=True)
        column = jnp.sum(jnp.where(col_id == j, a, 0.0), axis=1, keepdims=True)
        column = jnp.where(row_id > j, column, 0.0)
        scale = 1.0 / pivot
        big_a[...] = a - column * (row * scale)
        big_b[...] = inv - column * (inv_row * scale)
        return carry

    lax.fori_loop(0, size, eliminate, 0)
    diag = jnp.sum(jnp.where(here == there, big_a[...], 0.0), axis=1, keepdims=True)
    lower_inv = big_b[...] / jnp.sqrt(diag)

    wait_from(late_all, nslice, nb, recv.at[LATE_BAND])
    late_gram = jnp.sum(late_all[:nslice * nb, :].reshape(nslice, nb, LANES), axis=0)
    top = jnp.concatenate([tile_all[:nb, :size], late_gram[:, :size], tile_all[nb:2 * nb, :size]], axis=0)
    red_out[...] = dot(dot(lower_inv, full(top), NT), lower_inv, NT)

    wait_rows(gauge, (ng - 1) * rb, send.at[GA_OUT])
    wait_rows(gauge, (ng - 1) * rb, send.at[GA_BACK])
    wait_from(gauge, nslice, 5 * ROWS, send.at[SPREAD])
    wait_from(gauge, nslice, ROWS, send.at[LATE])

    @pl.when(b < nslice)
    def _():
        wait_from(late_in, ntile, ROWS, send.at[TILES])
        wait_rows(late_in, (ng - 1) * nb, send.at[LATE_GA])
        wait_rows(late_in, (nb - 1) * nb, send.at[LATE_BAND])

    @pl.when(b < ntile)
    def _():
        wait_rows(late_in, (ng - 1) * ROWS, send.at[TILE_SUM])
        wait_rows(late_in, (nb - 1) * ROWS, send.at[TILE_ALL])


def solution(mesh):
    nb, ng = mesh.shape["band"], mesh.shape["ga"]

    def shards(coef_x, coef_w, coef_p, hcoef_x, hcoef_p, potential, stick_column, sphere_mask):
        n = potential.shape[1]
        planes = potential.shape[0]
        sd = sphere_mask.shape[0]
        sp = n
        rb = 2 * planes
        half = n // 2
        cols = stick_column.reshape(ng * sd // n, n)
        size = 6 * nb
        ntile = 5 * nb // ROWS
        vmem = lambda *shape: pltpu.VMEM(shape, F32)
        scratch = [
            vmem(5, sd, n), vmem(2 * n, sp), vmem(2 * n, sp), pltpu.VMEM((ng, 2 * half, sp), BF16),
            vmem(2 * n, sp), vmem(2 * n, sp), vmem(5, nb * ROWS, n), vmem(ROWS, n),
            vmem(size, ROWS * n), vmem(5 * nb, LANES), vmem(nb * ROWS, LANES), vmem(ROWS, LANES),
            vmem(ng * ROWS, LANES), vmem(5 * nb, LANES), vmem(sd, n), vmem(nb * ROWS, n), vmem(nb, LANES),
            vmem(max(ng, nb) * nb, LANES), vmem(nb, LANES), vmem(nb * nb, LANES), vmem(size, size), vmem(size, size), vmem(sd, n),
            vmem(max(ng * rb, 5 * sd, nb * ROWS), n), pltpu.VMEM((4, ng // 4, n), jnp.int32),
            pltpu.SemaphoreType.DMA((9,)), pltpu.SemaphoreType.DMA((9,)), pltpu.SemaphoreType.DMA((15,)),
        ]
        forward, inverse, z_plus, y_plus, y_minus, z_minus, fx2 = [jnp.asarray(t) for t in tables(n, planes)]
        args = [coef_w, sphere_mask, forward, hcoef_x, hcoef_p, coef_x, coef_p, cols, fx2,
                z_plus, y_plus, potential, y_minus, z_minus, inverse]
        scratch = [pltpu.VMEM(a.shape, a.dtype) for a in args] + scratch
        return pl.pallas_call(
            functools.partial(kernel, n, nb, ng, sd, planes),
            out_shape=[jax.ShapeDtypeStruct(coef_w.shape, F32), jax.ShapeDtypeStruct((size, size), F32)],
            in_specs=[pl.BlockSpec(memory_space=pltpu.HBM)] * len(args),
            out_specs=[pl.BlockSpec(memory_space=pltpu.VMEM)] * 2,
            scratch_shapes=scratch,
            compiler_params=pltpu.CompilerParams(
                collective_id=0, has_side_effects=True, vmem_limit_bytes=60 * 1024 * 1024),
        )(*args)

    vec = P("band", "ga", None)
    in_specs = (vec, vec, vec, vec, vec, P("ga", None, None), P(), P("ga", None))
    return jax.shard_map(shards, mesh=mesh, in_specs=in_specs, out_specs=(vec, P()), check_vma=False)
```

```python
import functools
import math

import jax
import jax.numpy as jnp
import ml_dtypes
import numpy as np
from jax import lax
from jax.experimental import pallas as pl
from jax.experimental.pallas import tpu as pltpu
from jax.sharding import PartitionSpec as P

F32 = jnp.float32
BF16 = jnp.bfloat16
HI = lax.Precision.HIGHEST
ROWS = 8
LANES = 128
NT = (((1,), (1,)), ((), ()))
NN = (((1,), (0,)), ((), ()))
GA_OUT, GA_BACK, GROUP, MATES, EARLY, EARLY_GA, EARLY_BAND, LATE, LATE_GA, LATE_BAND = range(10)
TEAM = 4


def dot(a, b, dims=NN, precision=HI):
    return lax.dot_general(a, b, dims, precision=precision, preferred_element_type=F32)


def tables(n, planes):
    half, quarter = n // 2, n // 4
    lane = np.arange(n)
    is_real = (lane < quarter) | (lane >= n - quarter)
    k_of = np.where(is_real, lane, (lane - half) % n)
    fold_k = np.where(k_of < half, k_of, k_of - n)
    groups = n // planes
    x = (np.arange(groups)[:, None, None] * planes + np.arange(planes)[None, None, :]) + np.zeros((1, 2, 1), int)
    part = np.arange(2)[None, :, None] + np.zeros((groups, 1, planes), int)
    x, part = x.reshape(-1), part.reshape(-1)

    def angle(a, b):
        return 2.0 * math.pi * ((a[:, None] * b[None, :]) % n) / n

    th = angle(x, fold_k)
    c, s = np.cos(th), np.sin(th)
    pr = part[:, None] == 0
    ir = is_real[None, :]
    forward = np.where(pr, np.where(ir, c, -s), np.where(ir, s, c))
    inverse = np.where(pr, np.where(ir, c, -s), np.where(ir, s, c)) / float(n) ** 3
    small = np.arange(half)
    small = np.where(small < quarter, small, small - half)
    full = np.arange(n)
    th = angle(small, full)
    c, s = np.cos(th), np.sin(th)
    z_plus = np.concatenate([c, s], axis=1)
    y_plus = np.block([[c.T, -s.T], [s.T, c.T]])
    y_minus = np.block([[c, s], [-s, c]])
    z_real = np.concatenate([c.T, s.T], axis=0)
    z_imag = np.concatenate([-s.T, c.T], axis=0)
    z_minus = np.concatenate([z_real, z_real, z_imag, z_imag], axis=1)
    fx2 = (fold_k.astype(np.float64) ** 2)[None, :]
    pairs = []
    for t in (forward, inverse, z_plus, y_plus, y_minus, z_minus):
        high = t.astype(ml_dtypes.bfloat16)
        pairs.append(np.stack([high, (t - high.astype(np.float64)).astype(ml_dtypes.bfloat16)]))
    return pairs + [fx2.astype(np.float32)]


def kernel(n, nb, ng, sd, planes,
           coef_w_in, mask_in, forward_in, hcoef_x_in, hcoef_p_in, coef_x_in, coef_p_in, cols_in, fx2_in,
           z_plus_in, y_plus_in, pot_in, y_minus_in, z_minus_in, inverse_in,
           h_out, red_out,
           coef_w, mask, forward, hcoef_x, hcoef_p, coef_x, coef_p, cols, fx2,
           z_plus, y_plus, pot, y_minus, z_minus, inverse,
           src, ga_src, ga_in, hot, back_src, back_in, share, rows_src, ss_high, ss_low, early, early_in,
           early_mine, early_ga, early_all, hw, late, late_part, late_in, late_all, big_a, big_b, kin_ref, q_cols, send, recv, load):
    half, quarter = n // 2, n // 4
    rb = 2 * planes
    sp = hot.shape[2]
    cells = rb * half
    width = 3 * nb
    size = 2 * width
    part = sd // TEAM
    b = lax.axis_index("band")
    g = lax.axis_index("ga")
    seat = lax.rem(b, TEAM)
    team = b - seat
    lane = lax.broadcasted_iota(jnp.int32, (1, n), 1)
    real_lane = (lane < quarter) | (lane >= n - quarter)
    sign = jnp.where(real_lane, -1.0, 1.0).astype(F32)

    def swap(v):
        return pltpu.roll(v, half, 1)

    def pack(ref):
        v = ref[0]
        return jnp.where(real_lane, v[:, :n], swap(v[:, n:]))

    def rows(i, count=ROWS):
        return pl.ds(pl.multiple_of(i * count, count), count)

    def each(count, me, body):
        def step(k, carry):
            d = count // 2 + (k + 1) // 2 * (2 * lax.rem(k, 2) - 1)
            body(lax.rem(me + d, count))
            return carry
        lax.fori_loop(0, count - 1, step, 0)

    def push(src_ref, dst_ref, phase, where):
        pltpu.make_async_remote_copy(
            src_ref=src_ref, dst_ref=dst_ref, send_sem=send.at[phase], recv_sem=recv.at[phase],
            device_id=where, device_id_type=pl.DeviceIdType.MESH).start()

    def wait_for(piece, sem):
        pltpu.make_async_copy(piece, piece, sem).wait()

    def wait_rows(ref, count, sem):
        wait_for(ref.at[pl.ds(0, count)], sem)

    def split(v):
        high = v.astype(BF16)
        return high, (v - high.astype(F32)).astype(BF16)

    def dot3(a, b, dims=NN):
        return dot(a[0], b[0], dims, None) + (dot(a[0], b[1], dims, None) + dot(a[1], b[0], dims, None))

    def pair(table):
        return table[0], table[1]

    def gram(left, s_high, s_low):
        count = left.shape[0]
        high, low = split(left)
        upper = dot(jnp.concatenate([high, low], axis=0), s_high, NT, None)
        return upper[:count] + upper[count:] + dot(high, s_low, NT, None)

    held = [coef_w, mask, forward, hcoef_x, hcoef_p, coef_x, coef_p, cols, fx2,
            z_plus, y_plus, pot, y_minus, z_minus, inverse]
    given = [coef_w_in, mask_in, forward_in, hcoef_x_in, hcoef_p_in, coef_x_in, coef_p_in, cols_in, fx2_in,
             z_plus_in, y_plus_in, pot_in, y_minus_in, z_minus_in, inverse_in]
    loads = [pltpu.make_async_copy(a, v, load.at[i]) for i, (a, v) in enumerate(zip(given, held))]
    for copy in loads[:3]:
        copy.start()

    barrier = pltpu.get_barrier_semaphore()

    def greet_ga(p):
        pl.semaphore_signal(barrier, inc=1, device_id=(b, p), device_id_type=pl.DeviceIdType.MESH)

    def greet_band(p):
        pl.semaphore_signal(barrier, inc=1, device_id=(p, g), device_id_type=pl.DeviceIdType.MESH)

    each(ng, g, greet_ga)
    each(nb, b, greet_band)
    for copy in loads[3:]:
        copy.start()

    for copy in loads[:3]:
        copy.wait()
    m = mask[...].astype(F32)
    pm = jnp.where(real_lane, m, swap(m))
    w = pack(coef_w) * pm
    src[3] = w
    wide = jnp.concatenate([w, jnp.zeros((sp - sd, n), F32)], axis=0) if sp > sd else w
    ga_src[...] = dot3(pair(forward), split(wide), NT)
    pl.semaphore_wait(barrier, ng + nb - 2)

    def send_ga(p):
        push(ga_src.at[rows(p, rb)], ga_in.at[rows(g, rb)], GA_OUT, (b, p))

    each(ng, g, send_ga)
    ga_in[rows(g, rb), :] = ga_src[rows(g, rb), :]

    for copy in loads[3:7]:
        copy.wait()
    src[0] = pack(hcoef_x) * pm
    src[1] = pack(hcoef_p) * pm
    src[2] = pack(coef_x) * pm
    src[4] = pack(coef_p) * pm

    def seat_rows(p):
        return pl.ds(pl.multiple_of(p * part, ROWS), part)

    def send_group(p):
        push(src.at[pl.ds(2, 3), seat_rows(lax.rem(p, TEAM))], share.at[:, seat_rows(b)], GROUP, (p, g))

    each(nb, b, send_group)
    share[:, seat_rows(b), :] = src[2:5, seat_rows(seat), :]

    def each_mate(body):
        def step(d, carry):
            body(lax.rem(seat + d, TEAM))
            return carry
        lax.fori_loop(1, TEAM, step, 0)

    def send_mate(other):
        for a in range(2):
            push(src.at[a, seat_rows(other)], rows_src.at[seat_rows(a * TEAM + seat)], MATES, (team + other, g))

    each_mate(send_mate)
    for a in range(2):
        rows_src[seat_rows(a * TEAM + seat), :] = src[a, seat_rows(seat), :]

    for copy in loads[7:9]:
        copy.wait()

    fourth = n // 4
    strided = [cols[pl.ds(t, ng // 4, stride=3), :] for t in range(3)]
    lane32 = lax.broadcasted_iota(jnp.int32, (1, n), 1)
    q_cols[0] = strided[0]
    q_cols[1] = jnp.where(lane32 < fourth, pltpu.roll(strided[0], fourth, 1), pltpu.roll(strided[1], fourth, 1))
    q_cols[2] = jnp.where(lane32 < half, pltpu.roll(strided[1], half, 1), pltpu.roll(strided[2], half, 1))
    q_cols[3] = pltpu.roll(strided[2], 3 * fourth, 1)

    def cols_of(q):
        return q_cols[lax.rem(q, 4), pl.ds(q // 4, 1), :]

    def make_hot(q, carry):
        zc = cols_of(q) & (half - 1)
        one = jnp.where(lax.broadcasted_iota(jnp.int32, (half, sp), 0) == zc, 1.0, 0.0).astype(BF16)
        hot[q] = jnp.concatenate([one, one], axis=0)
        return carry

    lax.fori_loop(0, ng, make_hot, 0)

    def folded(v):
        return jnp.where(v < half, v, v - n)

    mine = cols_of(g)
    fy, fz = folded(mine // n), folded(mine & (n - 1))
    radial = jnp.broadcast_to((fy * fy + fz * fz).astype(F32), (n, sp)).T[:sd]
    kin_ref[...] = 0.5 * (2.0 * math.pi / n) ** 2 * (fx2[...] + radial)

    wait_rows(ga_in, (ng - 1) * rb, recv.at[GA_OUT])

    def y_hot(q):
        yc = (cols_of(q) // n) & (half - 1)
        return lax.broadcasted_iota(jnp.int32, (half, sp), 0) == yc

    group = 4 if ng % 4 == 0 else 2

    def scatter(i, acc):
        left, right = [], []
        for t in range(group):
            q = i * group + t
            v = ga_in[rows(q, rb), :]
            high = v.astype(BF16).astype(F32)
            low = v - high
            here = y_hot(q)[None]
            one = hot[q][:half]
            for piece in (high, low):
                spreadout = jnp.where(here, piece[:, None, :], 0.0).reshape(cells, sp)
                left.append(spreadout.astype(BF16))
                right.append(one)
        return acc + dot(jnp.concatenate(left, axis=1), jnp.concatenate(right, axis=1), NT, None)

    grid = lax.fori_loop(0, ng // group, scatter, jnp.zeros((cells, half), F32))

    for copy in loads[9:]:
        copy.wait()
    mid = planes * half
    turned = dot3(split(grid), pair(z_plus))
    f_re = turned[:mid, :n] - turned[mid:, n:]
    f_im = turned[:mid, n:] + turned[mid:, :n]
    stacked = jnp.concatenate(
        [jnp.concatenate([f_re[j * half:(j + 1) * half], f_im[j * half:(j + 1) * half]], axis=0)
         for j in range(planes)], axis=1)
    field = dot3(pair(y_plus), split(stacked))
    potential = jnp.concatenate([pot[j] for j in range(planes)], axis=1)
    product = jnp.concatenate([field[:n] * potential, field[n:] * potential], axis=0)
    product = dot3(pair(y_minus), split(product))
    product = jnp.concatenate(
        [jnp.concatenate([product[:half, j * n:(j + 1) * n], product[half:, j * n:(j + 1) * n]], axis=1)
         for j in range(planes)], axis=0)
    product = dot3(split(product), pair(z_minus))
    product = jnp.concatenate([product[:, :n], product[:, n:]], axis=0)
    high = product.astype(BF16).astype(F32)
    low = product - high
    both = jnp.where(lax.broadcasted_iota(jnp.int32, (1, n), 1) < half, high, low).astype(BF16)

    def gather(i, carry):
        pair = jnp.concatenate([hot[2 * i], hot[2 * i + 1]], axis=1)
        found = dot(both, pair, NN, None)
        for t in range(2):
            q = 2 * i + t
            here = y_hot(q)[None]
            part = found[:, t * sp:(t + 1) * sp].reshape(rb, half, sp)
            back_src[rows(q, rb), :] = jnp.sum(jnp.where(here, part, 0.0), axis=1)

            @pl.when(q != g)
            def _():
                push(back_src.at[rows(q, rb)], back_in.at[rows(g, rb)], GA_BACK, (b, q))
        return carry

    lax.fori_loop(0, ng // 2, gather, 0)
    back_in[rows(g, rb), :] = back_src[rows(g, rb), :]

    wait_for(share.at[:, pl.ds(0, (nb - 1) * part)], recv.at[GROUP])

    def make_span(i, carry):
        for t in range(3):
            r = i * 3 + t
            s = jnp.concatenate([share[a, pl.ds(r, nb, stride=part), :] for a in range(3)], axis=0)
            high, low = split(jnp.concatenate([s, swap(s) * sign], axis=0))
            at = pl.ds(pl.multiple_of(r * n, n), n)
            ss_high[:, at] = high
            ss_low[:, at] = low
        return carry

    lax.fori_loop(0, part // 3, make_span, 0)
    wait_rows(rows_src, 2 * (TEAM - 1) * part, recv.at[MATES])
    for a in range(3):
        rows_src[(2 + a) * TEAM * part:(3 + a) * TEAM * part] = share[a, pl.ds(pl.multiple_of(team * part, ROWS), TEAM * part), :]
    found = gram(jnp.concatenate([rows_src[pl.ds(r, 5 * TEAM, stride=part), :] for r in range(part)], axis=1),
                 ss_high[...], ss_low[...])
    for t in range(TEAM):
        for a in range(5):
            early[t, a, :, :size] = found[a * TEAM + t:a * TEAM + t + 1]

    def send_early(other):
        push(early.at[other], early_in.at[seat], EARLY, (team + other, g))

    each_mate(send_early)
    early_in[seat] = early[seat]
    wait_rows(early_in, TEAM - 1, recv.at[EARLY])
    early_mine[...] = jnp.sum(early_in[...], axis=0)

    def send_mine(p):
        push(early_mine, early_ga.at[g], EARLY_GA, (b, p))

    each(ng, g, send_mine)
    early_ga[g] = early_mine[...]
    wait_rows(back_in, (ng - 1) * rb, recv.at[GA_BACK])
    local = dot3(split(back_in[...].T), pair(inverse))[:sd]
    h = pm * (kin_ref[...] * w + local)
    hw[...] = h

    def send_late(other):
        push(hw.at[seat_rows(other)], late.at[seat_rows(seat)], LATE, (team + other, g))

    each_mate(send_late)
    late[seat_rows(seat), :] = hw[seat_rows(seat), :]

    h_out[0, :, :n] = jnp.where(real_lane, h, 0.0)
    h_out[0, :, n:] = jnp.where(real_lane, swap(h), 0.0)

    wait_rows(late, (TEAM - 1) * part, recv.at[LATE])
    found = gram(jnp.concatenate([late[pl.ds(r, TEAM, stride=part), :] for r in range(part)], axis=1),
                 ss_high[...], ss_low[...])
    for t in range(TEAM):
        late_part[t, :, :size] = found[t:t + 1]

    def send_part(p):
        push(late_part, late_in.at[g], LATE_GA, (b, p))

    each(ng, g, send_part)
    late_in[g] = late_part[...]

    wait_rows(early_ga, ng - 1, recv.at[EARLY_GA])
    early_all[b] = jnp.sum(early_ga[...], axis=0)

    def send_early_all(p):
        push(early_all.at[b], early_all.at[b], EARLY_BAND, (p, g))

    each(nb, b, send_early_all)


    wait_rows(late_in, ng - 1, recv.at[LATE_GA])
    late_all[b] = jnp.sum(late_in[...], axis=0)

    def send_whole(p):
        push(late_all.at[b], late_all.at[b], LATE_BAND, (p, g))

    each(nb, b, send_whole)

    wait_rows(early_all, nb - 1, recv.at[EARLY_BAND])

    def early_rows(a):
        return jnp.concatenate([early_all[p, a] for p in range(nb)], axis=0)[:, :size]

    def full(top):
        return jnp.concatenate(
            [top, jnp.concatenate([-top[:, width:2 * width], top[:, :width]], axis=1)], axis=0)

    big_a[...] = full(jnp.concatenate([early_rows(a) for a in range(2, 5)], axis=0))
    here = lax.broadcasted_iota(jnp.int32, (size, size), 0)
    there = lax.broadcasted_iota(jnp.int32, (size, size), 1)
    big_b[...] = jnp.where(here == there, 1.0, 0.0).astype(F32)
    row_id = lax.broadcasted_iota(jnp.int32, (size, 1), 0)
    col_id = lax.broadcasted_iota(jnp.int32, (1, size), 1)

    deep = 4

    def eliminate(i, carry):
        j = i * deep
        row = [big_a[pl.ds(j + m, 1), :] for m in range(deep)]
        inv_row = [big_b[pl.ds(j + m, 1), :] for m in range(deep)]
        a, inv = big_a[...], big_b[...]
        pivots = [[jnp.sum(jnp.where(col_id == j + q, row[m], 0.0), axis=1, keepdims=True) if q >= m else None
                   for q in range(deep)] for m in range(deep)]
        column = [jnp.sum(jnp.where(col_id == j + m, a, 0.0), axis=1, keepdims=True) for m in range(deep)]
        for m in range(deep):
            scale = 1.0 / pivots[m][m]
            for q in range(m + 1, deep):
                factor = pivots[m][q] * scale
                row[q] = row[q] - factor * row[m]
                inv_row[q] = inv_row[q] - factor * inv_row[m]
                column[q] = column[q] - factor * column[m]
                for t in range(q, deep):
                    pivots[q][t] = pivots[q][t] - factor * pivots[m][t]
            below = jnp.where(row_id > j + m, column[m], 0.0)
            a = a - below * (row[m] * scale)
            inv = inv - below * (inv_row[m] * scale)
        big_a[...] = a
        big_b[...] = inv
        return carry

    lax.fori_loop(0, size // deep, eliminate, 0)
    diag = jnp.sum(jnp.where(here == there, big_a[...], 0.0), axis=1, keepdims=True)
    lower_inv = big_b[...] / jnp.sqrt(diag)

    wait_rows(late_all, nb - 1, recv.at[LATE_BAND])
    late_gram = []
    for first in range(0, nb, TEAM):
        total = late_all[first]
        for t in range(1, TEAM):
            total = total + late_all[first + t]
        late_gram += [total[t] for t in range(TEAM)]
    late_gram = jnp.concatenate(late_gram, axis=0)
    top = jnp.concatenate([early_rows(0), late_gram[:, :size], early_rows(1)], axis=0)
    red_out[...] = dot(dot(lower_inv, full(top), NT), lower_inv, NT)

    wait_rows(ga_in, (ng - 1) * rb, send.at[GA_OUT])
    wait_rows(back_in, (ng - 1) * rb, send.at[GA_BACK])

    wait_for(share.at[:, pl.ds(0, (nb - 1) * part)], send.at[GROUP])
    wait_rows(rows_src, 2 * (TEAM - 1) * part, send.at[MATES])
    wait_rows(early_in, TEAM - 1, send.at[EARLY])
    wait_rows(early_ga, ng - 1, send.at[EARLY_GA])
    wait_rows(early_all, nb - 1, send.at[EARLY_BAND])
    wait_rows(late, (TEAM - 1) * part, send.at[LATE])
    wait_rows(late_in, ng - 1, send.at[LATE_GA])
    wait_rows(late_all, nb - 1, send.at[LATE_BAND])


def solution(mesh):
    nb, ng = mesh.shape["band"], mesh.shape["ga"]

    def shards(coef_x, coef_w, coef_p, hcoef_x, hcoef_p, potential, stick_column, sphere_mask):
        n = potential.shape[1]
        planes = potential.shape[0]
        sd = sphere_mask.shape[0]
        sp = n
        rb = 2 * planes
        half = n // 2
        cols = stick_column.reshape(ng * sd // n, n)
        size = 6 * nb
        part = sd // TEAM
        vmem = lambda *shape: pltpu.VMEM(shape, F32)
        scratch = [
            vmem(5, sd, n), vmem(2 * n, sp), vmem(2 * n, sp), pltpu.VMEM((ng, 2 * half, sp), BF16),
            vmem(2 * n, sp), vmem(2 * n, sp), vmem(3, nb * part, n), vmem(5 * TEAM * part, n),
            pltpu.VMEM((size, part * n), BF16),
            pltpu.VMEM((size, part * n), BF16), vmem(TEAM, 5, 1, LANES), vmem(TEAM, 5, 1, LANES),
            vmem(5, 1, LANES), vmem(ng, 5, 1, LANES), vmem(nb, 5, 1, LANES),
            vmem(sd, n), vmem(TEAM * part, n), vmem(TEAM, 1, LANES),
            vmem(ng, TEAM, 1, LANES), vmem(nb, TEAM, 1, LANES), vmem(size, size), vmem(size, size), vmem(sd, n),
            pltpu.VMEM((4, ng // 4, n), jnp.int32),
            pltpu.SemaphoreType.DMA((10,)), pltpu.SemaphoreType.DMA((10,)), pltpu.SemaphoreType.DMA((15,)),
        ]
        forward, inverse, z_plus, y_plus, y_minus, z_minus, fx2 = [jnp.asarray(t) for t in tables(n, planes)]
        args = [coef_w, sphere_mask, forward, hcoef_x, hcoef_p, coef_x, coef_p, cols, fx2,
                z_plus, y_plus, potential, y_minus, z_minus, inverse]
        scratch = [pltpu.VMEM(a.shape, a.dtype) for a in args] + scratch
        return pl.pallas_call(
            functools.partial(kernel, n, nb, ng, sd, planes),
            out_shape=[jax.ShapeDtypeStruct(coef_w.shape, F32), jax.ShapeDtypeStruct((size, size), F32)],
            in_specs=[pl.BlockSpec(memory_space=pltpu.HBM)] * len(args),
            out_specs=[pl.BlockSpec(memory_space=pltpu.VMEM)] * 2,
            scratch_shapes=scratch,
            compiler_params=pltpu.CompilerParams(
                collective_id=0, has_side_effects=True, vmem_limit_bytes=60 * 1024 * 1024),
        )(*args)

    vec = P("band", "ga", None)
    in_specs = (vec, vec, vec, vec, vec, P("ga", None, None), P(), P("ga", None))
    return jax.shard_map(shards, mesh=mesh, in_specs=in_specs, out_specs=(vec, P()), check_vma=False)
```

```python
import functools
import math

import jax
import jax.numpy as jnp
import ml_dtypes
import numpy as np
from jax import lax
from jax.experimental import pallas as pl
from jax.experimental.pallas import tpu as pltpu
from jax.sharding import PartitionSpec as P

F32 = jnp.float32
BF16 = jnp.bfloat16
HI = lax.Precision.HIGHEST
ROWS = 8
LANES = 128
NT = (((1,), (1,)), ((), ()))
NN = (((1,), (0,)), ((), ()))
GA_OUT, GA_BACK, GROUP, RELAY, MATES, EARLY, EARLY_GA, EARLY_BAND, LATE, LATE_GA, LATE_BAND = range(11)
TEAM = 4
ROW = 4


def dot(a, b, dims=NN, precision=HI):
    return lax.dot_general(a, b, dims, precision=precision, preferred_element_type=F32)


def tables(n, planes):
    half, quarter = n // 2, n // 4
    lane = np.arange(n)
    is_real = (lane < quarter) | (lane >= n - quarter)
    k_of = np.where(is_real, lane, (lane - half) % n)
    fold_k = np.where(k_of < half, k_of, k_of - n)
    groups = n // planes
    x = (np.arange(groups)[:, None, None] * planes + np.arange(planes)[None, None, :]) + np.zeros((1, 2, 1), int)
    part = np.arange(2)[None, :, None] + np.zeros((groups, 1, planes), int)
    x, part = x.reshape(-1), part.reshape(-1)

    def angle(a, b):
        return 2.0 * math.pi * ((a[:, None] * b[None, :]) % n) / n

    th = angle(x, fold_k)
    c, s = np.cos(th), np.sin(th)
    pr = part[:, None] == 0
    ir = is_real[None, :]
    forward = np.where(pr, np.where(ir, c, -s), np.where(ir, s, c))
    inverse = np.where(pr, np.where(ir, c, -s), np.where(ir, s, c)) / float(n) ** 3
    small = np.arange(half)
    small = np.where(small < quarter, small, small - half)
    full = np.arange(n)
    th = angle(small, full)
    c, s = np.cos(th), np.sin(th)
    z_plus = np.concatenate([c, s], axis=1)
    y_plus = np.block([[c.T, -s.T], [s.T, c.T]])
    y_minus = np.block([[c, s], [-s, c]])
    z_real = np.concatenate([c.T, s.T], axis=0)
    z_imag = np.concatenate([-s.T, c.T], axis=0)
    z_minus = np.concatenate([z_real, z_real, z_imag, z_imag], axis=1)
    fx2 = (fold_k.astype(np.float64) ** 2)[None, :]
    pairs = []
    for t in (forward, inverse, z_plus, y_plus, y_minus, z_minus):
        high = t.astype(ml_dtypes.bfloat16)
        pairs.append(np.stack([high, (t - high.astype(np.float64)).astype(ml_dtypes.bfloat16)]))
    return pairs + [fx2.astype(np.float32)]


def kernel(n, nb, ng, sd, planes,
           coef_w_in, mask_in, forward_in, hcoef_x_in, hcoef_p_in, coef_x_in, coef_p_in, cols_in, fx2_in,
           z_plus_in, y_plus_in, pot_in, y_minus_in, z_minus_in, inverse_in,
           h_out, red_out,
           coef_w, mask, forward, hcoef_x, hcoef_p, coef_x, coef_p, cols, fx2,
           z_plus, y_plus, pot, y_minus, z_minus, inverse,
           src, ga_src, ga_in, hot, back_src, back_in, share, rows_src, ss_high, ss_low, early, early_in,
           early_mine, early_ga, early_all, hw, late, late_part, late_in, late_all, big_a, big_b, kin_ref, q_cols, h_held, red_held, send, recv, load, near, store):
    half, quarter = n // 2, n // 4
    rb = 2 * planes
    sp = hot.shape[2]
    few = half // 4
    cells = rb * few
    width = 3 * nb
    size = 2 * width
    part = sd // TEAM
    b = lax.axis_index("band")
    g = lax.axis_index("ga")
    seat = lax.rem(b, TEAM)
    team = b - seat
    lane = lax.broadcasted_iota(jnp.int32, (1, n), 1)
    real_lane = (lane < quarter) | (lane >= n - quarter)
    sign = jnp.where(real_lane, -1.0, 1.0).astype(F32)

    def swap(v):
        return pltpu.roll(v, half, 1)

    def pack(ref):
        v = ref[0]
        return jnp.where(real_lane, v[:, :n], swap(v[:, n:]))

    def rows(i, count=ROWS):
        return pl.ds(pl.multiple_of(i * count, count), count)

    def each(count, me, body):
        def step(k, carry):
            d = count // 2 + (k + 1) // 2 * (2 * lax.rem(k, 2) - 1)
            body(lax.rem(me + d, count))
            return carry
        lax.fori_loop(0, count - 1, step, 0)

    def push(src_ref, dst_ref, phase, where, landed=None):
        pltpu.make_async_remote_copy(
            src_ref=src_ref, dst_ref=dst_ref, send_sem=send.at[phase],
            recv_sem=recv.at[phase] if landed is None else landed,
            device_id=where, device_id_type=pl.DeviceIdType.MESH).start()

    def wait_for(piece, sem):
        pltpu.make_async_copy(piece, piece, sem).wait()

    def wait_rows(ref, count, sem):
        wait_for(ref.at[pl.ds(0, count)], sem)

    def split(v):
        high = v.astype(BF16)
        return high, (v - high.astype(F32)).astype(BF16)

    def dot3(a, b, dims=NN):
        return dot(a[0], b[0], dims, None) + (dot(a[0], b[1], dims, None) + dot(a[1], b[0], dims, None))

    def pair(table):
        return table[0], table[1]

    def gram(left, s_high, s_low):
        count = left.shape[0]
        high, low = split(left)
        upper = dot(jnp.concatenate([high, low], axis=0), s_high, NT, None)
        return upper[:count] + upper[count:] + dot(high, s_low, NT, None)

    held = [coef_w, mask, forward, hcoef_x, hcoef_p, coef_x, coef_p, cols, fx2,
            z_plus, y_plus, pot, y_minus, z_minus, inverse]
    given = [coef_w_in, mask_in, forward_in, hcoef_x_in, hcoef_p_in, coef_x_in, coef_p_in, cols_in, fx2_in,
             z_plus_in, y_plus_in, pot_in, y_minus_in, z_minus_in, inverse_in]
    loads = [pltpu.make_async_copy(a, v, load.at[i]) for i, (a, v) in enumerate(zip(given, held))]
    for copy in loads[:3]:
        copy.start()

    barrier = pltpu.get_barrier_semaphore()

    def greet_ga(p):
        pl.semaphore_signal(barrier, inc=1, device_id=(b, p), device_id_type=pl.DeviceIdType.MESH)

    def greet_band(p):
        pl.semaphore_signal(barrier, inc=1, device_id=(p, g), device_id_type=pl.DeviceIdType.MESH)

    each(ng, g, greet_ga)
    each(nb, b, greet_band)
    for copy in loads[3:]:
        copy.start()

    for copy in loads[:3]:
        copy.wait()
    m = mask[...].astype(F32)
    pm = jnp.where(real_lane, m, swap(m))
    w = pack(coef_w) * pm
    src[3] = w
    wide = jnp.concatenate([w, jnp.zeros((sp - sd, n), F32)], axis=0) if sp > sd else w
    ga_src[...] = dot3(pair(forward), split(wide), NT)
    pl.semaphore_wait(barrier, ng + nb - 2)

    def send_ga(p):
        push(ga_src.at[rows(p, rb)], ga_in.at[rows(g, rb)], GA_OUT, (b, p), near.at[g // ROW])

    each(ng, g, send_ga)
    ga_in[rows(g, rb), :] = ga_src[rows(g, rb), :]

    for copy in loads[3:7]:
        copy.wait()
    src[0] = pack(hcoef_x) * pm
    src[1] = pack(hcoef_p) * pm
    src[2] = pack(coef_x) * pm
    src[4] = pack(coef_p) * pm

    def seat_rows(p):
        return pl.ds(pl.multiple_of(p * part, ROWS), part)

    chips = nb // 2
    chip, core = b // 2, lax.rem(b, 2)

    def chip_at(step):
        return lax.rem(chip + step + chips, chips)

    def send_group(p):
        push(src.at[pl.ds(2, 3), seat_rows(lax.rem(p, TEAM))], share.at[:, seat_rows(b)], GROUP, (p, g))

    for step in (2, -2, 1, -1):
        for c in range(2):
            send_group(2 * chip_at(step) + c)
    send_group(2 * chip + 1 - core)
    share[:, seat_rows(b), :] = src[2:5, seat_rows(seat), :]

    def each_mate(body):
        def step(d, carry):
            body(lax.rem(seat + d, TEAM))
            return carry
        lax.fori_loop(1, TEAM, step, 0)

    def send_mate(other):
        for a in range(2):
            push(src.at[a, seat_rows(other)], rows_src.at[seat_rows(a * TEAM + seat)], MATES, (team + other, g))

    each_mate(send_mate)
    for a in range(2):
        rows_src[seat_rows(a * TEAM + seat), :] = src[a, seat_rows(seat), :]

    def y_of(q):
        return (cols_of(q) // n) & (half - 1)

    for copy in loads[7:9]:
        copy.wait()

    fourth = n // 4
    strided = [cols[pl.ds(t, ng // 4, stride=3), :] for t in range(3)]
    lane32 = lax.broadcasted_iota(jnp.int32, (1, n), 1)
    q_cols[0] = strided[0]
    q_cols[1] = jnp.where(lane32 < fourth, pltpu.roll(strided[0], fourth, 1), pltpu.roll(strided[1], fourth, 1))
    q_cols[2] = jnp.where(lane32 < half, pltpu.roll(strided[1], half, 1), pltpu.roll(strided[2], half, 1))
    q_cols[3] = pltpu.roll(strided[2], 3 * fourth, 1)

    def cols_of(q):
        return q_cols[lax.rem(q, 4), pl.ds(q // 4, 1), :]

    def make_hot(q, carry):
        key = y_of(q) // few * half + (cols_of(q) & (half - 1))
        hot[q] = jnp.where(lax.broadcasted_iota(jnp.int32, (4 * half, sp), 0) == key, 1.0, 0.0).astype(BF16)
        return carry

    lax.fori_loop(0, ng, make_hot, 0)

    def folded(v):
        return jnp.where(v < half, v, v - n)

    mine = cols_of(g)
    fy, fz = folded(mine // n), folded(mine & (n - 1))
    radial = jnp.broadcast_to((fy * fy + fz * fz).astype(F32), (n, sp)).T[:sd]
    kin_ref[...] = 0.5 * (2.0 * math.pi / n) ** 2 * (fx2[...] + radial)

    nz = ng // ROW
    mz = g // ROW

    def row_at(i):
        return lax.rem(mz + (i + 1) // 2 * (2 * lax.rem(i, 2) - 1) + nz, nz)


    def y_hot(q):
        return lax.broadcasted_iota(jnp.int32, (few, sp), 0) == (y_of(q) & (few - 1))

    def scatter(i, acc):
        z = row_at(i)
        if isinstance(i, int):
            wait_rows(ga_in, (ROW - 1) * rb, near.at[z])
        else:
            wait_rows(ga_in, ROW * rb, near.at[z])
        upper, lower, right = [], [], []
        for t in range(ROW):
            q = z * ROW + t
            v = ga_in[rows(q, rb), :]
            high = v.astype(BF16).astype(F32)
            here = y_hot(q)[None]
            for piece, part_of in ((high, upper), (v - high, lower)):
                part_of.append(jnp.where(here, piece[:, None, :], 0.0).reshape(cells, sp).astype(BF16))
            right.append(hot[q])
        left = jnp.concatenate([jnp.concatenate(upper, axis=1), jnp.concatenate(lower, axis=1)], axis=0)
        return acc + dot(left, jnp.concatenate(right, axis=1), NT, None)

    grid = lax.fori_loop(1, nz, scatter, scatter(0, jnp.zeros((2 * cells, 4 * half), F32)))
    grid = grid[:cells] + grid[cells:]
    grid = jnp.concatenate(
        [grid[:, u * half:(u + 1) * half].reshape(rb, few, half) for u in range(4)], axis=1).reshape(rb * half, half)

    wait_for(share.at[:, pl.ds(0, 9 * part)], recv.at[GROUP])
    for way, last in ((1, 0), (-1, 1)):
        near_pair = pl.ds(pl.multiple_of(2 * chip_at(-way) * part, ROWS), 2 * part)
        for held_rows in (near_pair, seat_rows(2 * chip_at(-2 * way) + last)):
            push(share.at[:, held_rows], share.at[:, held_rows], RELAY, (2 * chip_at(2 * way) + core, g))

    for copy in loads[9:]:
        copy.wait()
    mid = planes * half
    turned = dot3(split(grid), pair(z_plus))
    f_re = turned[:mid, :n] - turned[mid:, n:]
    f_im = turned[:mid, n:] + turned[mid:, :n]
    stacked = jnp.concatenate(
        [jnp.concatenate([f_re[j * half:(j + 1) * half], f_im[j * half:(j + 1) * half]], axis=0)
         for j in range(planes)], axis=1)
    field = dot3(pair(y_plus), split(stacked))
    potential = jnp.concatenate([pot[j] for j in range(planes)], axis=1)
    product = jnp.concatenate([field[:n] * potential, field[n:] * potential], axis=0)
    product = dot3(pair(y_minus), split(product))
    product = jnp.concatenate(
        [jnp.concatenate([product[:half, j * n:(j + 1) * n], product[half:, j * n:(j + 1) * n]], axis=1)
         for j in range(planes)], axis=0)
    product = dot3(split(product), pair(z_minus))
    product = jnp.concatenate([product[:, :n], product[:, n:]], axis=0)
    product = product.reshape(rb, 4, few, 2 * half)
    left_lanes = lax.broadcasted_iota(jnp.int32, (1, n), 1) < half
    product = jnp.concatenate(
        [jnp.where(left_lanes, product[:, u].reshape(cells, n), product[:, u + 1].reshape(cells, n)) for u in (0, 2)],
        axis=1)
    both = jnp.concatenate(split(product), axis=0)

    def gather(i, carry):
        first = row_at(nz - 1 - i // 2) * ROW + 2 * lax.rem(i, 2)
        found = dot(both, jnp.concatenate([hot[first], hot[first + 1]], axis=1), NN, None)
        found = found[:cells] + found[cells:]
        for t in range(2):
            q = first + t
            here = y_hot(q)[None]
            part = found[:, t * sp:(t + 1) * sp].reshape(rb, few, sp)
            back_src[rows(q, rb), :] = jnp.sum(jnp.where(here, part, 0.0), axis=1)

            @pl.when(q != g)
            def _():
                push(back_src.at[rows(q, rb)], back_in.at[rows(g, rb)], GA_BACK, (b, q))
        return carry

    lax.fori_loop(0, ng // 2, gather, 0)
    back_in[rows(g, rb), :] = back_src[rows(g, rb), :]

    wait_for(share.at[:, pl.ds(0, 6 * part)], recv.at[RELAY])

    def make_span(i, carry):
        for t in range(3):
            r = i * 3 + t
            s = jnp.concatenate([share[a, pl.ds(r, nb, stride=part), :] for a in range(3)], axis=0)
            high, low = split(jnp.concatenate([s, swap(s) * sign], axis=0))
            at = pl.ds(pl.multiple_of(r * n, n), n)
            ss_high[:, at] = high
            ss_low[:, at] = low
        return carry

    lax.fori_loop(0, part // 3, make_span, 0)
    wait_rows(rows_src, 2 * (TEAM - 1) * part, recv.at[MATES])
    for a in range(3):
        rows_src[(2 + a) * TEAM * part:(3 + a) * TEAM * part] = share[a, pl.ds(pl.multiple_of(team * part, ROWS), TEAM * part), :]
    found = gram(jnp.concatenate([rows_src[pl.ds(r, 5 * TEAM, stride=part), :] for r in range(part)], axis=1),
                 ss_high[...], ss_low[...])
    for t in range(TEAM):
        for a in range(5):
            early[t, a, :, :size] = found[a * TEAM + t:a * TEAM + t + 1]

    def send_early(other):
        push(early.at[other], early_in.at[seat], EARLY, (team + other, g))

    each_mate(send_early)
    early_in[seat] = early[seat]
    wait_rows(back_in, (ng - 1) * rb, recv.at[GA_BACK])
    local = dot3(split(back_in[...].T), pair(inverse))[:sd]
    h = pm * (kin_ref[...] * w + local)
    hw[...] = h

    def send_late(other):
        push(hw.at[seat_rows(other)], late.at[seat_rows(seat)], LATE, (team + other, g))

    each_mate(send_late)
    late[seat_rows(seat), :] = hw[seat_rows(seat), :]

    h_held[0, :, :n] = jnp.where(real_lane, h, 0.0)
    h_held[0, :, n:] = jnp.where(real_lane, swap(h), 0.0)
    store_h = pltpu.make_async_copy(h_held, h_out, store.at[0])
    store_h.start()

    wait_rows(early_in, TEAM - 1, recv.at[EARLY])
    early_mine[...] = jnp.sum(early_in[...], axis=0)

    def send_mine(p):
        push(early_mine, early_ga.at[g], EARLY_GA, (b, p))

    each(ng, g, send_mine)
    early_ga[g] = early_mine[...]
    wait_rows(late, (TEAM - 1) * part, recv.at[LATE])
    found = gram(jnp.concatenate([late[pl.ds(r, TEAM, stride=part), :] for r in range(part)], axis=1),
                 ss_high[...], ss_low[...])
    for t in range(TEAM):
        late_part[t, :, :size] = found[t:t + 1]

    def send_part(p):
        push(late_part, late_in.at[g], LATE_GA, (b, p))

    each(ng, g, send_part)
    late_in[g] = late_part[...]

    wait_rows(early_ga, ng - 1, recv.at[EARLY_GA])
    early_all[b] = jnp.sum(early_ga[...], axis=0)

    def send_early_all(p):
        push(early_all.at[b], early_all.at[b], EARLY_BAND, (p, g))

    each(nb, b, send_early_all)


    wait_rows(late_in, ng - 1, recv.at[LATE_GA])
    late_all[b] = jnp.sum(late_in[...], axis=0)

    def send_whole(p):
        push(late_all.at[b], late_all.at[b], LATE_BAND, (p, g))

    each(nb, b, send_whole)

    wait_rows(early_all, nb - 1, recv.at[EARLY_BAND])

    def early_rows(a):
        return jnp.concatenate([early_all[p, a] for p in range(nb)], axis=0)[:, :size]

    def full(top):
        return jnp.concatenate(
            [top, jnp.concatenate([-top[:, width:2 * width], top[:, :width]], axis=1)], axis=0)

    big_a[...] = full(jnp.concatenate([early_rows(a) for a in range(2, 5)], axis=0))
    here = lax.broadcasted_iota(jnp.int32, (size, size), 0)
    there = lax.broadcasted_iota(jnp.int32, (size, size), 1)
    big_b[...] = jnp.where(here == there, 1.0, 0.0).astype(F32)
    row_id = lax.broadcasted_iota(jnp.int32, (size, 1), 0)
    col_id = lax.broadcasted_iota(jnp.int32, (1, size), 1)

    deep = 8

    def eliminate(top, i, carry):
        j = top + i * deep
        row = [big_a[pl.ds(j + m, 1), :] for m in range(deep)]
        inv_row = [big_b[pl.ds(j + m, 1), :] for m in range(deep)]
        a, inv = big_a[top:, :], big_b[top:, :]
        pivots = [[jnp.sum(jnp.where(col_id == j + q, row[m], 0.0), axis=1, keepdims=True) if q >= m else None
                   for q in range(deep)] for m in range(deep)]
        column = [jnp.sum(jnp.where(col_id == j + m, a, 0.0), axis=1, keepdims=True) for m in range(deep)]
        for m in range(deep):
            scale = 1.0 / pivots[m][m]
            for q in range(m + 1, deep):
                factor = pivots[m][q] * scale
                row[q] = row[q] - factor * row[m]
                inv_row[q] = inv_row[q] - factor * inv_row[m]
                column[q] = column[q] - factor * column[m]
                for t in range(q, deep):
                    pivots[q][t] = pivots[q][t] - factor * pivots[m][t]
            below = jnp.where(row_id[top:] > j + m, column[m], 0.0)
            a = a - below * (row[m] * scale)
            inv = inv - below * (inv_row[m] * scale)
        big_a[top:, :] = a
        big_b[top:, :] = inv
        return carry

    stretch = size // 6
    for top in range(0, size, stretch):
        lax.fori_loop(0, stretch // deep, functools.partial(eliminate, top), 0)
    diag = jnp.sum(jnp.where(here == there, big_a[...], 0.0), axis=1, keepdims=True)
    lower_inv = big_b[...] / jnp.sqrt(diag)

    wait_rows(late_all, nb - 1, recv.at[LATE_BAND])
    late_gram = []
    for first in range(0, nb, TEAM):
        total = late_all[first]
        for t in range(1, TEAM):
            total = total + late_all[first + t]
        late_gram += [total[t] for t in range(TEAM)]
    late_gram = jnp.concatenate(late_gram, axis=0)
    top = jnp.concatenate([early_rows(0), late_gram[:, :size], early_rows(1)], axis=0)
    red_held[...] = dot(dot(lower_inv, full(top), NT), lower_inv, NT)

    store_red = pltpu.make_async_copy(red_held, red_out, store.at[1])
    store_red.start()
    wait_rows(ga_in, (ng - 1) * rb, send.at[GA_OUT])
    wait_rows(back_in, (ng - 1) * rb, send.at[GA_BACK])

    wait_for(share.at[:, pl.ds(0, 9 * part)], send.at[GROUP])
    wait_for(share.at[:, pl.ds(0, 6 * part)], send.at[RELAY])
    wait_rows(rows_src, 2 * (TEAM - 1) * part, send.at[MATES])
    wait_rows(early_in, TEAM - 1, send.at[EARLY])
    wait_rows(early_ga, ng - 1, send.at[EARLY_GA])
    wait_rows(early_all, nb - 1, send.at[EARLY_BAND])
    wait_rows(late, (TEAM - 1) * part, send.at[LATE])
    wait_rows(late_in, ng - 1, send.at[LATE_GA])
    wait_rows(late_all, nb - 1, send.at[LATE_BAND])
    store_h.wait()
    store_red.wait()


def solution(mesh):
    nb, ng = mesh.shape["band"], mesh.shape["ga"]

    def shards(coef_x, coef_w, coef_p, hcoef_x, hcoef_p, potential, stick_column, sphere_mask):
        n = potential.shape[1]
        planes = potential.shape[0]
        sd = sphere_mask.shape[0]
        sp = n
        rb = 2 * planes
        half = n // 2
        cols = stick_column.reshape(ng * sd // n, n)
        size = 6 * nb
        part = sd // TEAM
        vmem = lambda *shape: pltpu.VMEM(shape, F32)
        scratch = [
            vmem(5, sd, n), vmem(2 * n, sp), vmem(2 * n, sp), pltpu.VMEM((ng, 4 * half, sp), BF16),
            vmem(2 * n, sp), vmem(2 * n, sp), vmem(3, nb * part, n), vmem(5 * TEAM * part, n),
            pltpu.VMEM((size, part * n), BF16),
            pltpu.VMEM((size, part * n), BF16), vmem(TEAM, 5, 1, LANES), vmem(TEAM, 5, 1, LANES),
            vmem(5, 1, LANES), vmem(ng, 5, 1, LANES), vmem(nb, 5, 1, LANES),
            vmem(sd, n), vmem(TEAM * part, n), vmem(TEAM, 1, LANES),
            vmem(ng, TEAM, 1, LANES), vmem(nb, TEAM, 1, LANES), vmem(size, size), vmem(size, size), vmem(sd, n),
            pltpu.VMEM((4, ng // 4, n), jnp.int32),
            vmem(1, sd, 2 * n), vmem(size, size),
            pltpu.SemaphoreType.DMA((11,)), pltpu.SemaphoreType.DMA((11,)), pltpu.SemaphoreType.DMA((15,)),
            pltpu.SemaphoreType.DMA((ng // ROW,)), pltpu.SemaphoreType.DMA((2,)),
        ]
        forward, inverse, z_plus, y_plus, y_minus, z_minus, fx2 = [jnp.asarray(t) for t in tables(n, planes)]
        args = [coef_w, sphere_mask, forward, hcoef_x, hcoef_p, coef_x, coef_p, cols, fx2,
                z_plus, y_plus, potential, y_minus, z_minus, inverse]
        scratch = [pltpu.VMEM(a.shape, a.dtype) for a in args] + scratch
        return pl.pallas_call(
            functools.partial(kernel, n, nb, ng, sd, planes),
            out_shape=[jax.ShapeDtypeStruct(coef_w.shape, F32), jax.ShapeDtypeStruct((size, size), F32)],
            in_specs=[pl.BlockSpec(memory_space=pltpu.HBM)] * len(args),
            out_specs=[pl.BlockSpec(memory_space=pltpu.HBM)] * 2,
            scratch_shapes=scratch,
            compiler_params=pltpu.CompilerParams(
                collective_id=0, has_side_effects=True, vmem_limit_bytes=60 * 1024 * 1024),
        )(*args)

    vec = P("band", "ga", None)
    in_specs = (vec, vec, vec, vec, vec, P("ga", None, None), P(), P("ga", None))
    return jax.shard_map(shards, mesh=mesh, in_specs=in_specs, out_specs=(vec, P()), check_vma=False)
```

```python
import functools
import math

import jax
import jax.numpy as jnp
import ml_dtypes
import numpy as np
from jax import lax
from jax.experimental import pallas as pl
from jax.experimental.pallas import tpu as pltpu
from jax.sharding import PartitionSpec as P

F32 = jnp.float32
BF16 = jnp.bfloat16
HI = lax.Precision.HIGHEST
ROWS = 8
LANES = 128
NT = (((1,), (1,)), ((), ()))
NN = (((1,), (0,)), ((), ()))
GA_OUT, GA_BACK, GROUP, RELAY, MATES, EARLY, EARLY_GA, EARLY_BAND, LATE, LATE_GA, LATE_BAND = range(11)
TEAM = 4
ROW = 4


def dot(a, b, dims=NN, precision=HI):
    return lax.dot_general(a, b, dims, precision=precision, preferred_element_type=F32)


def tables(n, planes):
    half, quarter = n // 2, n // 4
    lane = np.arange(n)
    is_real = (lane < quarter) | (lane >= n - quarter)
    k_of = np.where(is_real, lane, (lane - half) % n)
    fold_k = np.where(k_of < half, k_of, k_of - n)
    groups = n // planes
    x = (np.arange(groups)[:, None, None] * planes + np.arange(planes)[None, None, :]) + np.zeros((1, 2, 1), int)
    part = np.arange(2)[None, :, None] + np.zeros((groups, 1, planes), int)
    x, part = x.reshape(-1), part.reshape(-1)

    def angle(a, b):
        return 2.0 * math.pi * ((a[:, None] * b[None, :]) % n) / n

    th = angle(x, fold_k)
    c, s = np.cos(th), np.sin(th)
    pr = part[:, None] == 0
    ir = is_real[None, :]
    forward = np.where(pr, np.where(ir, c, -s), np.where(ir, s, c))
    inverse = np.where(pr, np.where(ir, c, -s), np.where(ir, s, c)) / float(n) ** 3
    small = np.arange(half)
    small = np.where(small < quarter, small, small - half)
    full = np.arange(n)
    th = angle(small, full)
    c, s = np.cos(th), np.sin(th)
    z_plus = np.concatenate([c, s], axis=1)
    y_plus = np.block([[c.T, -s.T], [s.T, c.T]])
    y_minus = np.block([[c, s], [-s, c]])
    z_real = np.concatenate([c.T, s.T], axis=0)
    z_imag = np.concatenate([-s.T, c.T], axis=0)
    z_minus = np.concatenate([z_real, z_real, z_imag, z_imag], axis=1)
    fx2 = (fold_k.astype(np.float64) ** 2)[None, :]
    pairs = []
    for t in (forward, inverse, z_plus, y_plus, y_minus, z_minus):
        high = t.astype(ml_dtypes.bfloat16)
        pairs.append(np.stack([high, (t - high.astype(np.float64)).astype(ml_dtypes.bfloat16)]))
    return pairs + [fx2.astype(np.float32)]


def kernel(n, nb, ng, sd, planes,
           coef_w_in, mask_in, forward_in, hcoef_x_in, hcoef_p_in, coef_x_in, coef_p_in, cols_in, fx2_in,
           z_plus_in, y_plus_in, pot_in, y_minus_in, z_minus_in, inverse_in,
           h_out, red_out,
           coef_w, mask, forward, hcoef_x, hcoef_p, coef_x, coef_p, cols, fx2,
           z_plus, y_plus, pot, y_minus, z_minus, inverse,
           src, ga_src, ga_in, hot, back_src, back_in, share, rows_src, ss_high, ss_low, early, early_in,
           early_mine, early_ga, early_all, hw, late, late_part, late_in, late_all, big_a, big_b, kin_ref, q_cols, h_held, red_held, send, recv, load, near, store):
    half, quarter = n // 2, n // 4
    rb = 2 * planes
    sp = hot.shape[2]
    few = half // 4
    cells = rb * few
    width = 3 * nb
    size = 2 * width
    part = sd // TEAM
    b = lax.axis_index("band")
    g = lax.axis_index("ga")
    seat = lax.rem(b, TEAM)
    team = b - seat
    lane = lax.broadcasted_iota(jnp.int32, (1, n), 1)
    real_lane = (lane < quarter) | (lane >= n - quarter)
    sign = jnp.where(real_lane, -1.0, 1.0).astype(F32)

    def swap(v):
        return pltpu.roll(v, half, 1)

    def pack(ref):
        v = ref[0]
        return jnp.where(real_lane, v[:, :n], swap(v[:, n:]))

    def rows(i, count=ROWS):
        return pl.ds(pl.multiple_of(i * count, count), count)

    def each(count, me, body):
        def step(k, carry):
            d = count // 2 + (k + 1) // 2 * (2 * lax.rem(k, 2) - 1)
            body(lax.rem(me + d, count))
            return carry
        lax.fori_loop(0, count - 1, step, 0)

    def push(src_ref, dst_ref, phase, where, landed=None):
        pltpu.make_async_remote_copy(
            src_ref=src_ref, dst_ref=dst_ref, send_sem=send.at[phase],
            recv_sem=recv.at[phase] if landed is None else landed,
            device_id=where, device_id_type=pl.DeviceIdType.MESH).start()

    def wait_for(piece, sem):
        pltpu.make_async_copy(piece, piece, sem).wait()

    def wait_rows(ref, count, sem):
        wait_for(ref.at[pl.ds(0, count)], sem)

    def split(v):
        high = v.astype(BF16)
        return high, (v - high.astype(F32)).astype(BF16)

    def dot3(a, b, dims=NN):
        return dot(a[0], b[0], dims, None) + (dot(a[0], b[1], dims, None) + dot(a[1], b[0], dims, None))

    def pair(table):
        return table[0], table[1]

    def gram(left, s_high, s_low):
        count = left.shape[0]
        high, low = split(left)
        upper = dot(jnp.concatenate([high, low], axis=0), s_high, NT, None)
        return upper[:count] + upper[count:] + dot(high, s_low, NT, None)

    held = [coef_w, mask, forward, hcoef_x, hcoef_p, coef_x, coef_p, cols, fx2,
            z_plus, y_plus, pot, y_minus, z_minus, inverse]
    given = [coef_w_in, mask_in, forward_in, hcoef_x_in, hcoef_p_in, coef_x_in, coef_p_in, cols_in, fx2_in,
             z_plus_in, y_plus_in, pot_in, y_minus_in, z_minus_in, inverse_in]
    loads = [pltpu.make_async_copy(a, v, load.at[i]) for i, (a, v) in enumerate(zip(given, held))]
    for copy in loads[:3]:
        copy.start()

    barrier = pltpu.get_barrier_semaphore()

    def greet_ga(p):
        pl.semaphore_signal(barrier, inc=1, device_id=(b, p), device_id_type=pl.DeviceIdType.MESH)

    def greet_band(p):
        pl.semaphore_signal(barrier, inc=1, device_id=(p, g), device_id_type=pl.DeviceIdType.MESH)

    each(ng, g, greet_ga)
    each(nb, b, greet_band)
    for copy in loads[3:]:
        copy.start()

    for copy in loads[:3]:
        copy.wait()
    m = mask[...].astype(F32)
    pm = jnp.where(real_lane, m, swap(m))
    w = pack(coef_w) * pm
    src[3] = w
    wide = jnp.concatenate([w, jnp.zeros((sp - sd, n), F32)], axis=0) if sp > sd else w
    ga_src[...] = dot3(pair(forward), split(wide), NT)
    for copy in loads[3:7]:
        copy.wait()
    src[0] = pack(hcoef_x) * pm
    src[1] = pack(hcoef_p) * pm
    src[2] = pack(coef_x) * pm
    src[4] = pack(coef_p) * pm

    pl.semaphore_wait(barrier, ng + nb - 2)

    def seat_rows(p):
        return pl.ds(pl.multiple_of(p * part, ROWS), part)

    chips = nb // 2
    chip, core = b // 2, lax.rem(b, 2)

    def chip_at(step):
        return lax.rem(chip + step + chips, chips)

    def send_group(p):
        push(src.at[pl.ds(2, 3), seat_rows(lax.rem(p, TEAM))], share.at[:, seat_rows(b)], GROUP, (p, g))

    for step in (2, -2, 1, -1):
        for c in range(2):
            send_group(2 * chip_at(step) + c)
    send_group(2 * chip + 1 - core)
    share[:, seat_rows(b), :] = src[2:5, seat_rows(seat), :]

    def send_ga(p):
        push(ga_src.at[rows(p, rb)], ga_in.at[rows(g, rb)], GA_OUT, (b, p), near.at[g // ROW])

    each(ng, g, send_ga)
    ga_in[rows(g, rb), :] = ga_src[rows(g, rb), :]

    def each_mate(body):
        def step(d, carry):
            body(lax.rem(seat + d, TEAM))
            return carry
        lax.fori_loop(1, TEAM, step, 0)

    def send_mate(other):
        for a in range(2):
            push(src.at[a, seat_rows(other)], rows_src.at[seat_rows(a * TEAM + seat)], MATES, (team + other, g))

    each_mate(send_mate)
    for a in range(2):
        rows_src[seat_rows(a * TEAM + seat), :] = src[a, seat_rows(seat), :]

    def y_of(q):
        return (cols_of(q) // n) & (half - 1)

    for copy in loads[7:9]:
        copy.wait()

    fourth = n // 4
    strided = [cols[pl.ds(t, ng // 4, stride=3), :] for t in range(3)]
    lane32 = lax.broadcasted_iota(jnp.int32, (1, n), 1)
    q_cols[0] = strided[0]
    q_cols[1] = jnp.where(lane32 < fourth, pltpu.roll(strided[0], fourth, 1), pltpu.roll(strided[1], fourth, 1))
    q_cols[2] = jnp.where(lane32 < half, pltpu.roll(strided[1], half, 1), pltpu.roll(strided[2], half, 1))
    q_cols[3] = pltpu.roll(strided[2], 3 * fourth, 1)

    def cols_of(q):
        return q_cols[lax.rem(q, 4), pl.ds(q // 4, 1), :]

    def make_hot(q, carry):
        key = y_of(q) // few * half + (cols_of(q) & (half - 1))
        hot[q] = jnp.where(lax.broadcasted_iota(jnp.int32, (4 * half, sp), 0) == key, 1.0, 0.0).astype(BF16)
        return carry

    lax.fori_loop(0, ng, make_hot, 0)

    def folded(v):
        return jnp.where(v < half, v, v - n)

    mine = cols_of(g)
    fy, fz = folded(mine // n), folded(mine & (n - 1))
    radial = jnp.broadcast_to((fy * fy + fz * fz).astype(F32), (n, sp)).T[:sd]
    kin_ref[...] = 0.5 * (2.0 * math.pi / n) ** 2 * (fx2[...] + radial)

    nz = ng // ROW
    mz = g // ROW

    def row_at(i):
        return lax.rem(mz + (i + 1) // 2 * (2 * lax.rem(i, 2) - 1) + nz, nz)


    def y_hot(q):
        return lax.broadcasted_iota(jnp.int32, (few, sp), 0) == (y_of(q) & (few - 1))

    def scatter(i, acc):
        z = row_at(i)
        if isinstance(i, int):
            wait_rows(ga_in, (ROW - 1) * rb, near.at[z])
        else:
            wait_rows(ga_in, ROW * rb, near.at[z])
        upper, lower, right = [], [], []
        for t in range(ROW):
            q = z * ROW + t
            v = ga_in[rows(q, rb), :]
            high = v.astype(BF16).astype(F32)
            here = y_hot(q)[None]
            for piece, part_of in ((high, upper), (v - high, lower)):
                part_of.append(jnp.where(here, piece[:, None, :], 0.0).reshape(cells, sp).astype(BF16))
            right.append(hot[q])
        left = jnp.concatenate([jnp.concatenate(upper, axis=1), jnp.concatenate(lower, axis=1)], axis=0)
        return acc + dot(left, jnp.concatenate(right, axis=1), NT, None)

    grid = lax.fori_loop(1, nz, scatter, scatter(0, jnp.zeros((2 * cells, 4 * half), F32)))
    grid = grid[:cells] + grid[cells:]
    grid = jnp.concatenate(
        [grid[:, u * half:(u + 1) * half].reshape(rb, few, half) for u in range(4)], axis=1).reshape(rb * half, half)

    wait_for(share.at[:, pl.ds(0, 9 * part)], recv.at[GROUP])
    for way, last in ((1, 0), (-1, 1)):
        near_pair = pl.ds(pl.multiple_of(2 * chip_at(-way) * part, ROWS), 2 * part)
        for held_rows in (near_pair, seat_rows(2 * chip_at(-2 * way) + last)):
            push(share.at[:, held_rows], share.at[:, held_rows], RELAY, (2 * chip_at(2 * way) + core, g))

    for copy in loads[9:]:
        copy.wait()
    mid = planes * half
    turned = dot3(split(grid), pair(z_plus))
    f_re = turned[:mid, :n] - turned[mid:, n:]
    f_im = turned[:mid, n:] + turned[mid:, :n]
    stacked = jnp.concatenate(
        [jnp.concatenate([f_re[j * half:(j + 1) * half], f_im[j * half:(j + 1) * half]], axis=0)
         for j in range(planes)], axis=1)
    field = dot3(pair(y_plus), split(stacked))
    potential = jnp.concatenate([pot[j] for j in range(planes)], axis=1)
    product = jnp.concatenate([field[:n] * potential, field[n:] * potential], axis=0)
    product = dot3(pair(y_minus), split(product))
    product = jnp.concatenate(
        [jnp.concatenate([product[:half, j * n:(j + 1) * n], product[half:, j * n:(j + 1) * n]], axis=1)
         for j in range(planes)], axis=0)
    product = dot3(split(product), pair(z_minus))
    product = jnp.concatenate([product[:, :n], product[:, n:]], axis=0)
    product = product.reshape(rb, 4, few, 2 * half)
    left_lanes = lax.broadcasted_iota(jnp.int32, (1, n), 1) < half
    product = jnp.concatenate(
        [jnp.where(left_lanes, product[:, u].reshape(cells, n), product[:, u + 1].reshape(cells, n)) for u in (0, 2)],
        axis=1)
    both = jnp.concatenate(split(product), axis=0)

    def gather(i, carry):
        first = row_at(nz - 1 - i // 2) * ROW + 2 * lax.rem(i, 2)
        found = dot(both, jnp.concatenate([hot[first], hot[first + 1]], axis=1), NN, None)
        found = found[:cells] + found[cells:]
        for t in range(2):
            q = first + t
            here = y_hot(q)[None]
            part = found[:, t * sp:(t + 1) * sp].reshape(rb, few, sp)
            back_src[rows(q, rb), :] = jnp.sum(jnp.where(here, part, 0.0), axis=1)

            @pl.when(q != g)
            def _():
                push(back_src.at[rows(q, rb)], back_in.at[rows(g, rb)], GA_BACK, (b, q))
        return carry

    lax.fori_loop(0, ng // 2, gather, 0)
    back_in[rows(g, rb), :] = back_src[rows(g, rb), :]

    wait_for(share.at[:, pl.ds(0, 6 * part)], recv.at[RELAY])

    def make_span(i, carry):
        for t in range(3):
            r = i * 3 + t
            s = jnp.concatenate([share[a, pl.ds(r, nb, stride=part), :] for a in range(3)], axis=0)
            high, low = split(jnp.concatenate([s, swap(s) * sign], axis=0))
            at = pl.ds(pl.multiple_of(r * n, n), n)
            ss_high[:, at] = high
            ss_low[:, at] = low
        return carry

    lax.fori_loop(0, part // 3, make_span, 0)
    wait_rows(rows_src, 2 * (TEAM - 1) * part, recv.at[MATES])
    for a in range(3):
        rows_src[(2 + a) * TEAM * part:(3 + a) * TEAM * part] = share[a, pl.ds(pl.multiple_of(team * part, ROWS), TEAM * part), :]
    found = gram(jnp.concatenate([rows_src[pl.ds(r, 5 * TEAM, stride=part), :] for r in range(part)], axis=1),
                 ss_high[...], ss_low[...])
    for t in range(TEAM):
        for a in range(5):
            early[t, a, :, :size] = found[a * TEAM + t:a * TEAM + t + 1]

    def send_early(other):
        push(early.at[other], early_in.at[seat], EARLY, (team + other, g))

    each_mate(send_early)
    early_in[seat] = early[seat]
    wait_rows(back_in, (ng - 1) * rb, recv.at[GA_BACK])
    local = dot3(split(back_in[...].T), pair(inverse))[:sd]
    h = pm * (kin_ref[...] * w + local)
    hw[...] = h

    def send_late(other):
        push(hw.at[seat_rows(other)], late.at[seat_rows(seat)], LATE, (team + other, g))

    each_mate(send_late)
    late[seat_rows(seat), :] = hw[seat_rows(seat), :]

    h_held[0, :, :n] = jnp.where(real_lane, h, 0.0)
    h_held[0, :, n:] = jnp.where(real_lane, swap(h), 0.0)
    store_h = pltpu.make_async_copy(h_held, h_out, store.at[0])
    store_h.start()

    wait_rows(early_in, TEAM - 1, recv.at[EARLY])
    early_mine[...] = jnp.sum(early_in[...], axis=0)

    def send_mine(p):
        push(early_mine, early_ga.at[g], EARLY_GA, (b, p))

    each(ng, g, send_mine)
    early_ga[g] = early_mine[...]
    wait_rows(late, (TEAM - 1) * part, recv.at[LATE])
    found = gram(jnp.concatenate([late[pl.ds(r, TEAM, stride=part), :] for r in range(part)], axis=1),
                 ss_high[...], ss_low[...])
    for t in range(TEAM):
        late_part[t, :, :size] = found[t:t + 1]

    def send_part(p):
        push(late_part, late_in.at[g], LATE_GA, (b, p))

    each(ng, g, send_part)
    late_in[g] = late_part[...]

    wait_rows(early_ga, ng - 1, recv.at[EARLY_GA])
    early_all[b] = jnp.sum(early_ga[...], axis=0)

    def send_early_all(p):
        push(early_all.at[b], early_all.at[b], EARLY_BAND, (p, g))

    each(nb, b, send_early_all)


    wait_rows(late_in, ng - 1, recv.at[LATE_GA])
    late_all[b] = jnp.sum(late_in[...], axis=0)

    def send_whole(p):
        push(late_all.at[b], late_all.at[b], LATE_BAND, (p, g))

    each(nb, b, send_whole)

    wait_rows(early_all, nb - 1, recv.at[EARLY_BAND])

    def early_rows(a):
        return jnp.concatenate([early_all[p, a] for p in range(nb)], axis=0)[:, :size]

    def full(top):
        return jnp.concatenate(
            [top, jnp.concatenate([-top[:, width:2 * width], top[:, :width]], axis=1)], axis=0)

    big_a[...] = full(jnp.concatenate([early_rows(a) for a in range(2, 5)], axis=0))
    here = lax.broadcasted_iota(jnp.int32, (size, size), 0)
    there = lax.broadcasted_iota(jnp.int32, (size, size), 1)
    big_b[...] = jnp.where(here == there, 1.0, 0.0).astype(F32)
    row_id = lax.broadcasted_iota(jnp.int32, (size, 1), 0)
    col_id = lax.broadcasted_iota(jnp.int32, (1, size), 1)

    deep = 8

    def eliminate(top, i, carry):
        j = top + i * deep
        row = [big_a[pl.ds(j + m, 1), :] for m in range(deep)]
        inv_row = [big_b[pl.ds(j + m, 1), :] for m in range(deep)]
        a, inv = big_a[top:, :], big_b[top:, :]
        pivots = [[jnp.sum(jnp.where(col_id == j + q, row[m], 0.0), axis=1, keepdims=True) if q >= m else None
                   for q in range(deep)] for m in range(deep)]
        column = [jnp.sum(jnp.where(col_id == j + m, a, 0.0), axis=1, keepdims=True) for m in range(deep)]
        for m in range(deep):
            scale = 1.0 / pivots[m][m]
            for q in range(m + 1, deep):
                factor = pivots[m][q] * scale
                row[q] = row[q] - factor * row[m]
                inv_row[q] = inv_row[q] - factor * inv_row[m]
                column[q] = column[q] - factor * column[m]
                for t in range(q, deep):
                    pivots[q][t] = pivots[q][t] - factor * pivots[m][t]
            below = jnp.where(row_id[top:] > j + m, column[m], 0.0)
            a = a - below * (row[m] * scale)
            inv = inv - below * (inv_row[m] * scale)
        big_a[top:, :] = a
        big_b[top:, :] = inv
        return carry

    stretch = size // 6
    for top in range(0, size, stretch):
        lax.fori_loop(0, stretch // deep, functools.partial(eliminate, top), 0)
    diag = jnp.sum(jnp.where(here == there, big_a[...], 0.0), axis=1, keepdims=True)
    lower_inv = split(big_b[...] / jnp.sqrt(diag))
    h_x, h_p = early_rows(0), early_rows(1)

    wait_rows(late_all, nb - 1, recv.at[LATE_BAND])
    late_gram = []
    for first in range(0, nb, TEAM):
        total = late_all[first]
        for t in range(1, TEAM):
            total = total + late_all[first + t]
        late_gram += [total[t] for t in range(TEAM)]
    late_gram = jnp.concatenate(late_gram, axis=0)
    top = jnp.concatenate([h_x, late_gram[:, :size], h_p], axis=0)
    red_held[...] = dot3(split(dot3(lower_inv, split(full(top)), NT)), lower_inv, NT)

    store_red = pltpu.make_async_copy(red_held, red_out, store.at[1])
    store_red.start()
    wait_rows(ga_in, (ng - 1) * rb, send.at[GA_OUT])
    wait_rows(back_in, (ng - 1) * rb, send.at[GA_BACK])

    wait_for(share.at[:, pl.ds(0, 9 * part)], send.at[GROUP])
    wait_for(share.at[:, pl.ds(0, 6 * part)], send.at[RELAY])
    wait_rows(rows_src, 2 * (TEAM - 1) * part, send.at[MATES])
    wait_rows(early_in, TEAM - 1, send.at[EARLY])
    wait_rows(early_ga, ng - 1, send.at[EARLY_GA])
    wait_rows(early_all, nb - 1, send.at[EARLY_BAND])
    wait_rows(late, (TEAM - 1) * part, send.at[LATE])
    wait_rows(late_in, ng - 1, send.at[LATE_GA])
    wait_rows(late_all, nb - 1, send.at[LATE_BAND])
    store_h.wait()
    store_red.wait()


def solution(mesh):
    nb, ng = mesh.shape["band"], mesh.shape["ga"]

    def shards(coef_x, coef_w, coef_p, hcoef_x, hcoef_p, potential, stick_column, sphere_mask):
        n = potential.shape[1]
        planes = potential.shape[0]
        sd = sphere_mask.shape[0]
        sp = n
        rb = 2 * planes
        half = n // 2
        cols = stick_column.reshape(ng * sd // n, n)
        size = 6 * nb
        part = sd // TEAM
        vmem = lambda *shape: pltpu.VMEM(shape, F32)
        scratch = [
            vmem(5, sd, n), vmem(2 * n, sp), vmem(2 * n, sp), pltpu.VMEM((ng, 4 * half, sp), BF16),
            vmem(2 * n, sp), vmem(2 * n, sp), vmem(3, nb * part, n), vmem(5 * TEAM * part, n),
            pltpu.VMEM((size, part * n), BF16),
            pltpu.VMEM((size, part * n), BF16), vmem(TEAM, 5, 1, LANES), vmem(TEAM, 5, 1, LANES),
            vmem(5, 1, LANES), vmem(ng, 5, 1, LANES), vmem(nb, 5, 1, LANES),
            vmem(sd, n), vmem(TEAM * part, n), vmem(TEAM, 1, LANES),
            vmem(ng, TEAM, 1, LANES), vmem(nb, TEAM, 1, LANES), vmem(size, size), vmem(size, size), vmem(sd, n),
            pltpu.VMEM((4, ng // 4, n), jnp.int32),
            vmem(1, sd, 2 * n), vmem(size, size),
            pltpu.SemaphoreType.DMA((11,)), pltpu.SemaphoreType.DMA((11,)), pltpu.SemaphoreType.DMA((15,)),
            pltpu.SemaphoreType.DMA((ng // ROW,)), pltpu.SemaphoreType.DMA((2,)),
        ]
        forward, inverse, z_plus, y_plus, y_minus, z_minus, fx2 = [jnp.asarray(t) for t in tables(n, planes)]
        args = [coef_w, sphere_mask, forward, hcoef_x, hcoef_p, coef_x, coef_p, cols, fx2,
                z_plus, y_plus, potential, y_minus, z_minus, inverse]
        scratch = [pltpu.VMEM(a.shape, a.dtype) for a in args] + scratch
        return pl.pallas_call(
            functools.partial(kernel, n, nb, ng, sd, planes),
            out_shape=[jax.ShapeDtypeStruct(coef_w.shape, F32), jax.ShapeDtypeStruct((size, size), F32)],
            in_specs=[pl.BlockSpec(memory_space=pltpu.HBM)] * len(args),
            out_specs=[pl.BlockSpec(memory_space=pltpu.HBM)] * 2,
            scratch_shapes=scratch,
            compiler_params=pltpu.CompilerParams(
                collective_id=0, has_side_effects=True, vmem_limit_bytes=60 * 1024 * 1024),
        )(*args)

    vec = P("band", "ga", None)
    in_specs = (vec, vec, vec, vec, vec, P("ga", None, None), P(), P("ga", None))
    return jax.shard_map(shards, mesh=mesh, in_specs=in_specs, out_specs=(vec, P()), check_vma=False)
```

```python
import functools
import math

import jax
import jax.numpy as jnp
import ml_dtypes
import numpy as np
from jax import lax
from jax.experimental import pallas as pl
from jax.experimental.pallas import tpu as pltpu
from jax.sharding import PartitionSpec as P

F32 = jnp.float32
BF16 = jnp.bfloat16
HI = lax.Precision.HIGHEST
ROWS = 8
LANES = 128
NT = (((1,), (1,)), ((), ()))
NN = (((1,), (0,)), ((), ()))
GA_OUT, GA_BACK, GROUP, RELAY, MATES, EARLY, EARLY_GA, EARLY_BAND, LATE, LATE_GA, LATE_BAND = range(11)
TEAM = 4
ROW = 4


def dot(a, b, dims=NN, precision=HI):
    return lax.dot_general(a, b, dims, precision=precision, preferred_element_type=F32)


def tables(n, planes):
    half, quarter = n // 2, n // 4
    lane = np.arange(n)
    is_real = (lane < quarter) | (lane >= n - quarter)
    k_of = np.where(is_real, lane, (lane - half) % n)
    fold_k = np.where(k_of < half, k_of, k_of - n)
    groups = n // planes
    x = (np.arange(groups)[:, None, None] * planes + np.arange(planes)[None, None, :]) + np.zeros((1, 2, 1), int)
    part = np.arange(2)[None, :, None] + np.zeros((groups, 1, planes), int)
    x, part = x.reshape(-1), part.reshape(-1)

    def angle(a, b):
        return 2.0 * math.pi * ((a[:, None] * b[None, :]) % n) / n

    th = angle(x, fold_k)
    c, s = np.cos(th), np.sin(th)
    pr = part[:, None] == 0
    ir = is_real[None, :]
    forward = np.where(pr, np.where(ir, c, -s), np.where(ir, s, c))
    inverse = np.where(pr, np.where(ir, c, -s), np.where(ir, s, c)) / float(n) ** 3
    small = np.arange(half)
    small = np.where(small < quarter, small, small - half)
    full = np.arange(n)
    th = angle(small, full)
    c, s = np.cos(th), np.sin(th)
    z_plus = np.concatenate([c, s], axis=1)
    y_plus = np.block([[c.T, -s.T], [s.T, c.T]])
    y_minus = np.block([[c, s], [-s, c]])
    z_real = np.concatenate([c.T, s.T], axis=0)
    z_imag = np.concatenate([-s.T, c.T], axis=0)
    z_minus = np.concatenate([z_real, z_real, z_imag, z_imag], axis=1)
    fx2 = (fold_k.astype(np.float64) ** 2)[None, :]
    pairs = []
    for t in (forward, inverse, z_plus, y_plus, y_minus, z_minus):
        high = t.astype(ml_dtypes.bfloat16)
        pairs.append(np.stack([high, (t - high.astype(np.float64)).astype(ml_dtypes.bfloat16)]))
    return pairs + [fx2.astype(np.float32)]


def kernel(n, nb, ng, sd, planes,
           coef_w_in, mask_in, forward_in, hcoef_x_in, hcoef_p_in, coef_x_in, coef_p_in, cols_in, fx2_in,
           z_plus_in, y_plus_in, pot_in, y_minus_in, z_minus_in, inverse_in,
           h_out, red_out,
           coef_w, mask, forward, hcoef_x, hcoef_p, coef_x, coef_p, cols, fx2,
           z_plus, y_plus, pot, y_minus, z_minus, inverse,
           src, ga_src, ga_in, hot, back_src, back_in, share, rows_src, ss, early, early_in,
           early_mine, early_ga, early_all, hw, late, late_part, late_in, late_all, big_a, big_b, kin_ref, q_cols, h_held, red_held, send, recv, load, near, store):
    half, quarter = n // 2, n // 4
    rb = 2 * planes
    sp = hot.shape[2]
    few = half // 4
    cells = rb * few
    width = 3 * nb
    size = 2 * width
    part = sd // TEAM
    b = lax.axis_index("band")
    g = lax.axis_index("ga")
    seat = lax.rem(b, TEAM)
    team = b - seat
    lane = lax.broadcasted_iota(jnp.int32, (1, n), 1)
    real_lane = (lane < quarter) | (lane >= n - quarter)
    sign = jnp.where(real_lane, -1.0, 1.0).astype(F32)

    def swap(v):
        return pltpu.roll(v, half, 1)

    def pack(ref):
        v = ref[0]
        return jnp.where(real_lane, v[:, :n], swap(v[:, n:]))

    def rows(i, count=ROWS):
        return pl.ds(pl.multiple_of(i * count, count), count)

    def each(count, me, body):
        def step(k, carry):
            d = count // 2 + (k + 1) // 2 * (2 * lax.rem(k, 2) - 1)
            body(lax.rem(me + d, count))
            return carry
        lax.fori_loop(0, count - 1, step, 0)

    def push(src_ref, dst_ref, phase, where, landed=None):
        pltpu.make_async_remote_copy(
            src_ref=src_ref, dst_ref=dst_ref, send_sem=send.at[phase],
            recv_sem=recv.at[phase] if landed is None else landed,
            device_id=where, device_id_type=pl.DeviceIdType.MESH).start()

    def wait_for(piece, sem):
        pltpu.make_async_copy(piece, piece, sem).wait()

    def wait_rows(ref, count, sem):
        wait_for(ref.at[pl.ds(0, count)], sem)

    def split(v):
        high = v.astype(BF16)
        return high, (v - high.astype(F32)).astype(BF16)

    def dot3(a, b, dims=NN):
        return dot(a[0], b[0], dims, None) + (dot(a[0], b[1], dims, None) + dot(a[1], b[0], dims, None))

    def pair(table):
        return table[0], table[1]

    def gram(left):
        count = left.shape[0]
        found = dot(jnp.concatenate(split(left), axis=0), ss[...], NT, None)
        return found[:count, :size] + found[count:, :size] + found[:count, size:]

    held = [coef_w, mask, forward, hcoef_x, hcoef_p, coef_x, coef_p, cols, fx2,
            z_plus, y_plus, pot, y_minus, z_minus, inverse]
    given = [coef_w_in, mask_in, forward_in, hcoef_x_in, hcoef_p_in, coef_x_in, coef_p_in, cols_in, fx2_in,
             z_plus_in, y_plus_in, pot_in, y_minus_in, z_minus_in, inverse_in]
    loads = [pltpu.make_async_copy(a, v, load.at[i]) for i, (a, v) in enumerate(zip(given, held))]
    for copy in loads[:3]:
        copy.start()

    barrier = pltpu.get_barrier_semaphore()

    def greet_ga(p):
        pl.semaphore_signal(barrier, inc=1, device_id=(b, p), device_id_type=pl.DeviceIdType.MESH)

    def greet_band(p):
        pl.semaphore_signal(barrier, inc=1, device_id=(p, g), device_id_type=pl.DeviceIdType.MESH)

    each(ng, g, greet_ga)
    each(nb, b, greet_band)
    for copy in loads[3:]:
        copy.start()

    for copy in loads[:3]:
        copy.wait()
    m = mask[...].astype(F32)
    pm = jnp.where(real_lane, m, swap(m))
    w = pack(coef_w) * pm
    src[3] = w
    wide = jnp.concatenate([w, jnp.zeros((sp - sd, n), F32)], axis=0) if sp > sd else w
    ga_src[...] = dot3(pair(forward), split(wide), NT)
    for copy in loads[3:7]:
        copy.wait()
    src[0] = pack(hcoef_x) * pm
    src[1] = pack(hcoef_p) * pm
    src[2] = pack(coef_x) * pm
    src[4] = pack(coef_p) * pm

    pl.semaphore_wait(barrier, ng + nb - 2)

    def seat_rows(p):
        return pl.ds(pl.multiple_of(p * part, ROWS), part)

    chips = nb // 2
    chip, core = b // 2, lax.rem(b, 2)

    def chip_at(step):
        return lax.rem(chip + step + chips, chips)

    def send_group(p):
        push(src.at[pl.ds(2, 3), seat_rows(lax.rem(p, TEAM))], share.at[:, seat_rows(b)], GROUP, (p, g))

    for step in (2, -2, 1, -1):
        for c in range(2):
            send_group(2 * chip_at(step) + c)
    send_group(2 * chip + 1 - core)
    share[:, seat_rows(b), :] = src[2:5, seat_rows(seat), :]

    def send_ga(p):
        push(ga_src.at[rows(p, rb)], ga_in.at[rows(g, rb)], GA_OUT, (b, p), near.at[g // ROW])

    each(ng, g, send_ga)
    ga_in[rows(g, rb), :] = ga_src[rows(g, rb), :]

    def each_mate(body):
        def step(d, carry):
            body(lax.rem(seat + d, TEAM))
            return carry
        lax.fori_loop(1, TEAM, step, 0)

    def send_mate(other):
        for a in range(2):
            push(src.at[a, seat_rows(other)], rows_src.at[seat_rows(a * TEAM + seat)], MATES, (team + other, g))

    each_mate(send_mate)
    for a in range(2):
        rows_src[seat_rows(a * TEAM + seat), :] = src[a, seat_rows(seat), :]

    def y_of(q):
        return (cols_of(q) // n) & (half - 1)

    for copy in loads[7:9]:
        copy.wait()

    fourth = n // 4
    strided = [cols[pl.ds(t, ng // 4, stride=3), :] for t in range(3)]
    lane32 = lax.broadcasted_iota(jnp.int32, (1, n), 1)
    q_cols[0] = strided[0]
    q_cols[1] = jnp.where(lane32 < fourth, pltpu.roll(strided[0], fourth, 1), pltpu.roll(strided[1], fourth, 1))
    q_cols[2] = jnp.where(lane32 < half, pltpu.roll(strided[1], half, 1), pltpu.roll(strided[2], half, 1))
    q_cols[3] = pltpu.roll(strided[2], 3 * fourth, 1)

    def cols_of(q):
        return q_cols[lax.rem(q, 4), pl.ds(q // 4, 1), :]

    def make_hot(q, carry):
        key = y_of(q) // few * half + (cols_of(q) & (half - 1))
        hot[q] = jnp.where(lax.broadcasted_iota(jnp.int32, (4 * half, sp), 0) == key, 1.0, 0.0).astype(BF16)
        return carry

    lax.fori_loop(0, ng, make_hot, 0)

    def folded(v):
        return jnp.where(v < half, v, v - n)

    mine = cols_of(g)
    fy, fz = folded(mine // n), folded(mine & (n - 1))
    radial = jnp.broadcast_to((fy * fy + fz * fz).astype(F32), (n, sp)).T[:sd]
    kin_ref[...] = 0.5 * (2.0 * math.pi / n) ** 2 * (fx2[...] + radial)

    nz = ng // ROW
    mz = g // ROW

    def row_at(i):
        return lax.rem(mz + (i + 1) // 2 * (2 * lax.rem(i, 2) - 1) + nz, nz)


    def y_hot(q):
        return lax.broadcasted_iota(jnp.int32, (few, sp), 0) == (y_of(q) & (few - 1))

    def scatter(i, acc):
        z = row_at(i)
        if isinstance(i, int):
            wait_rows(ga_in, (ROW - 1) * rb, near.at[z])
        else:
            wait_rows(ga_in, ROW * rb, near.at[z])
        upper, lower, right = [], [], []
        for t in range(ROW):
            q = z * ROW + t
            v = ga_in[rows(q, rb), :]
            high = v.astype(BF16).astype(F32)
            here = y_hot(q)[None]
            for piece, part_of in ((high, upper), (v - high, lower)):
                part_of.append(jnp.where(here, piece[:, None, :], 0.0).reshape(cells, sp).astype(BF16))
            right.append(hot[q])
        left = jnp.concatenate([jnp.concatenate(upper, axis=1), jnp.concatenate(lower, axis=1)], axis=0)
        return acc + dot(left, jnp.concatenate(right, axis=1), NT, None)

    grid = lax.fori_loop(1, nz, scatter, scatter(0, jnp.zeros((2 * cells, 4 * half), F32)))
    grid = grid[:cells] + grid[cells:]
    grid = jnp.concatenate(
        [grid[:, u * half:(u + 1) * half].reshape(rb, few, half) for u in range(4)], axis=1).reshape(rb * half, half)

    wait_for(share.at[:, pl.ds(0, 9 * part)], recv.at[GROUP])
    for way, last in ((1, 0), (-1, 1)):
        near_pair = pl.ds(pl.multiple_of(2 * chip_at(-way) * part, ROWS), 2 * part)
        for held_rows in (near_pair, seat_rows(2 * chip_at(-2 * way) + last)):
            push(share.at[:, held_rows], share.at[:, held_rows], RELAY, (2 * chip_at(2 * way) + core, g))

    for copy in loads[9:]:
        copy.wait()
    mid = planes * half
    turned = dot3(split(grid), pair(z_plus))
    f_re = turned[:mid, :n] - turned[mid:, n:]
    f_im = turned[:mid, n:] + turned[mid:, :n]
    stacked = jnp.concatenate(
        [jnp.concatenate([f_re[j * half:(j + 1) * half], f_im[j * half:(j + 1) * half]], axis=0)
         for j in range(planes)], axis=1)
    field = dot3(pair(y_plus), split(stacked))
    potential = jnp.concatenate([pot[j] for j in range(planes)], axis=1)
    product = jnp.concatenate([field[:n] * potential, field[n:] * potential], axis=0)
    product = dot3(pair(y_minus), split(product))
    product = jnp.concatenate(
        [jnp.concatenate([product[:half, j * n:(j + 1) * n], product[half:, j * n:(j + 1) * n]], axis=1)
         for j in range(planes)], axis=0)
    product = dot3(split(product), pair(z_minus))
    product = jnp.concatenate([product[:, :n], product[:, n:]], axis=0)
    product = product.reshape(rb, 4, few, 2 * half)
    left_lanes = lax.broadcasted_iota(jnp.int32, (1, n), 1) < half
    product = jnp.concatenate(
        [jnp.where(left_lanes, product[:, u].reshape(cells, n), product[:, u + 1].reshape(cells, n)) for u in (0, 2)],
        axis=1)
    both = jnp.concatenate(split(product), axis=0)

    def gather(i, carry):
        first = row_at(nz - 1 - i // 2) * ROW + 2 * lax.rem(i, 2)
        found = dot(both, jnp.concatenate([hot[first], hot[first + 1]], axis=1), NN, None)
        found = found[:cells] + found[cells:]
        for t in range(2):
            q = first + t
            here = y_hot(q)[None]
            part = found[:, t * sp:(t + 1) * sp].reshape(rb, few, sp)
            back_src[rows(q, rb), :] = jnp.sum(jnp.where(here, part, 0.0), axis=1)

            @pl.when(q != g)
            def _():
                push(back_src.at[rows(q, rb)], back_in.at[rows(g, rb)], GA_BACK, (b, q))
        return carry

    lax.fori_loop(0, ng // 2, gather, 0)
    back_in[rows(g, rb), :] = back_src[rows(g, rb), :]

    wait_for(share.at[:, pl.ds(0, 6 * part)], recv.at[RELAY])

    def make_span(i, carry):
        for t in range(3):
            r = i * 3 + t
            s = jnp.concatenate([share[a, pl.ds(r, nb, stride=part), :] for a in range(3)], axis=0)
            high, low = split(jnp.concatenate([s, swap(s) * sign], axis=0))
            at = pl.ds(pl.multiple_of(r * n, n), n)
            ss[:size, at] = high
            ss[size:, at] = low
        return carry

    lax.fori_loop(0, part // 3, make_span, 0)
    wait_rows(rows_src, 2 * (TEAM - 1) * part, recv.at[MATES])
    for a in range(3):
        rows_src[(2 + a) * TEAM * part:(3 + a) * TEAM * part] = share[a, pl.ds(pl.multiple_of(team * part, ROWS), TEAM * part), :]
    found = gram(jnp.concatenate([rows_src[pl.ds(r, 5 * TEAM, stride=part), :] for r in range(part)], axis=1))
    for t in range(TEAM):
        for a in range(5):
            early[t, a, :, :size] = found[a * TEAM + t:a * TEAM + t + 1]

    def send_early(other):
        push(early.at[other], early_in.at[seat], EARLY, (team + other, g))

    each_mate(send_early)
    early_in[seat] = early[seat]
    wait_rows(back_in, (ng - 1) * rb, recv.at[GA_BACK])
    local = dot3(split(back_in[...].T), pair(inverse))[:sd]
    h = pm * (kin_ref[...] * w + local)
    hw[...] = h

    def send_late(other):
        push(hw.at[seat_rows(other)], late.at[seat_rows(seat)], LATE, (team + other, g))

    each_mate(send_late)
    late[seat_rows(seat), :] = hw[seat_rows(seat), :]

    h_held[0, :, :n] = jnp.where(real_lane, h, 0.0)
    h_held[0, :, n:] = jnp.where(real_lane, swap(h), 0.0)
    store_h = pltpu.make_async_copy(h_held, h_out, store.at[0])
    store_h.start()

    wait_rows(early_in, TEAM - 1, recv.at[EARLY])
    early_mine[...] = jnp.sum(early_in[...], axis=0)

    def send_mine(p):
        push(early_mine, early_ga.at[g], EARLY_GA, (b, p))

    each(ng, g, send_mine)
    early_ga[g] = early_mine[...]
    wait_rows(late, (TEAM - 1) * part, recv.at[LATE])
    found = gram(jnp.concatenate([late[pl.ds(r, TEAM, stride=part), :] for r in range(part)], axis=1))
    for t in range(TEAM):
        late_part[t, :, :size] = found[t:t + 1]

    def send_part(p):
        push(late_part, late_in.at[g], LATE_GA, (b, p))

    each(ng, g, send_part)
    late_in[g] = late_part[...]

    wait_rows(early_ga, ng - 1, recv.at[EARLY_GA])
    early_all[b] = jnp.sum(early_ga[...], axis=0)

    def send_early_all(p):
        push(early_all.at[b], early_all.at[b], EARLY_BAND, (p, g))

    each(nb, b, send_early_all)


    wait_rows(late_in, ng - 1, recv.at[LATE_GA])
    late_all[b] = jnp.sum(late_in[...], axis=0)

    def send_whole(p):
        push(late_all.at[b], late_all.at[b], LATE_BAND, (p, g))

    each(nb, b, send_whole)

    wait_rows(early_all, nb - 1, recv.at[EARLY_BAND])

    def early_rows(a):
        return jnp.concatenate([early_all[p, a] for p in range(nb)], axis=0)[:, :size]

    def full(top):
        return jnp.concatenate(
            [top, jnp.concatenate([-top[:, width:2 * width], top[:, :width]], axis=1)], axis=0)

    big_a[...] = full(jnp.concatenate([early_rows(a) for a in range(2, 5)], axis=0))
    here = lax.broadcasted_iota(jnp.int32, (size, size), 0)
    there = lax.broadcasted_iota(jnp.int32, (size, size), 1)
    big_b[...] = jnp.where(here == there, 1.0, 0.0).astype(F32)
    row_id = lax.broadcasted_iota(jnp.int32, (size, 1), 0)
    col_id = lax.broadcasted_iota(jnp.int32, (1, size), 1)

    deep = 8

    def eliminate(top, i, carry):
        j = top + i * deep
        row = [big_a[pl.ds(j + m, 1), :] for m in range(deep)]
        inv_row = [big_b[pl.ds(j + m, 1), :] for m in range(deep)]
        a, inv = big_a[top:, :], big_b[top:, :]
        pivots = [[jnp.sum(jnp.where(col_id == j + q, row[m], 0.0), axis=1, keepdims=True) if q >= m else None
                   for q in range(deep)] for m in range(deep)]
        column = [jnp.sum(jnp.where(col_id == j + m, a, 0.0), axis=1, keepdims=True) for m in range(deep)]
        for m in range(deep):
            scale = 1.0 / pivots[m][m]
            for q in range(m + 1, deep):
                factor = pivots[m][q] * scale
                row[q] = row[q] - factor * row[m]
                inv_row[q] = inv_row[q] - factor * inv_row[m]
                column[q] = column[q] - factor * column[m]
                for t in range(q, deep):
                    pivots[q][t] = pivots[q][t] - factor * pivots[m][t]
            below = jnp.where(row_id[top:] > j + m, column[m], 0.0)
            a = a - below * (row[m] * scale)
            inv = inv - below * (inv_row[m] * scale)
        big_a[top:, :] = a
        big_b[top:, :] = inv
        return carry

    stretch = size // 6
    for top in range(0, size, stretch):
        lax.fori_loop(0, stretch // deep, functools.partial(eliminate, top), 0)
    diag = jnp.sum(jnp.where(here == there, big_a[...], 0.0), axis=1, keepdims=True)
    lower_inv = split(big_b[...] / jnp.sqrt(diag))
    h_x, h_p = early_rows(0), early_rows(1)

    wait_rows(late_all, nb - 1, recv.at[LATE_BAND])
    late_gram = []
    for first in range(0, nb, TEAM):
        total = late_all[first]
        for t in range(1, TEAM):
            total = total + late_all[first + t]
        late_gram += [total[t] for t in range(TEAM)]
    late_gram = jnp.concatenate(late_gram, axis=0)
    top = jnp.concatenate([h_x, late_gram[:, :size], h_p], axis=0)
    red_held[...] = dot3(split(dot3(lower_inv, split(full(top)), NT)), lower_inv, NT)

    store_red = pltpu.make_async_copy(red_held, red_out, store.at[1])
    store_red.start()
    wait_rows(ga_in, (ng - 1) * rb, send.at[GA_OUT])
    wait_rows(back_in, (ng - 1) * rb, send.at[GA_BACK])

    wait_for(share.at[:, pl.ds(0, 9 * part)], send.at[GROUP])
    wait_for(share.at[:, pl.ds(0, 6 * part)], send.at[RELAY])
    wait_rows(rows_src, 2 * (TEAM - 1) * part, send.at[MATES])
    wait_rows(early_in, TEAM - 1, send.at[EARLY])
    wait_rows(early_ga, ng - 1, send.at[EARLY_GA])
    wait_rows(early_all, nb - 1, send.at[EARLY_BAND])
    wait_rows(late, (TEAM - 1) * part, send.at[LATE])
    wait_rows(late_in, ng - 1, send.at[LATE_GA])
    wait_rows(late_all, nb - 1, send.at[LATE_BAND])
    store_h.wait()
    store_red.wait()


def solution(mesh):
    nb, ng = mesh.shape["band"], mesh.shape["ga"]

    def shards(coef_x, coef_w, coef_p, hcoef_x, hcoef_p, potential, stick_column, sphere_mask):
        n = potential.shape[1]
        planes = potential.shape[0]
        sd = sphere_mask.shape[0]
        sp = n
        rb = 2 * planes
        half = n // 2
        cols = stick_column.reshape(ng * sd // n, n)
        size = 6 * nb
        part = sd // TEAM
        vmem = lambda *shape: pltpu.VMEM(shape, F32)
        scratch = [
            vmem(5, sd, n), vmem(2 * n, sp), vmem(2 * n, sp), pltpu.VMEM((ng, 4 * half, sp), BF16),
            vmem(2 * n, sp), vmem(2 * n, sp), vmem(3, nb * part, n), vmem(5 * TEAM * part, n),
            pltpu.VMEM((2 * size, part * n), BF16),
            vmem(TEAM, 5, 1, LANES), vmem(TEAM, 5, 1, LANES),
            vmem(5, 1, LANES), vmem(ng, 5, 1, LANES), vmem(nb, 5, 1, LANES),
            vmem(sd, n), vmem(TEAM * part, n), vmem(TEAM, 1, LANES),
            vmem(ng, TEAM, 1, LANES), vmem(nb, TEAM, 1, LANES), vmem(size, size), vmem(size, size), vmem(sd, n),
            pltpu.VMEM((4, ng // 4, n), jnp.int32),
            vmem(1, sd, 2 * n), vmem(size, size),
            pltpu.SemaphoreType.DMA((11,)), pltpu.SemaphoreType.DMA((11,)), pltpu.SemaphoreType.DMA((15,)),
            pltpu.SemaphoreType.DMA((ng // ROW,)), pltpu.SemaphoreType.DMA((2,)),
        ]
        forward, inverse, z_plus, y_plus, y_minus, z_minus, fx2 = [jnp.asarray(t) for t in tables(n, planes)]
        args = [coef_w, sphere_mask, forward, hcoef_x, hcoef_p, coef_x, coef_p, cols, fx2,
                z_plus, y_plus, potential, y_minus, z_minus, inverse]
        scratch = [pltpu.VMEM(a.shape, a.dtype) for a in args] + scratch
        return pl.pallas_call(
            functools.partial(kernel, n, nb, ng, sd, planes),
            out_shape=[jax.ShapeDtypeStruct(coef_w.shape, F32), jax.ShapeDtypeStruct((size, size), F32)],
            in_specs=[pl.BlockSpec(memory_space=pltpu.HBM)] * len(args),
            out_specs=[pl.BlockSpec(memory_space=pltpu.HBM)] * 2,
            scratch_shapes=scratch,
            compiler_params=pltpu.CompilerParams(
                collective_id=0, has_side_effects=True, vmem_limit_bytes=60 * 1024 * 1024),
        )(*args)

    vec = P("band", "ga", None)
    in_specs = (vec, vec, vec, vec, vec, P("ga", None, None), P(), P("ga", None))
    return jax.shard_map(shards, mesh=mesh, in_specs=in_specs, out_specs=(vec, P()), check_vma=False)
```
